32 devices in a mesh: groups: 2 (over x), tile: 16 (over z, y, core).
Axes of the slice: x: 2, y: 2, z: 4, core: 2. Of those that a mesh axis runs over, the one named last changes fastest.
Arguments:
- latent_rows: bfloat16 [4096, 256], P(('groups', 'tile')), parts along dimension 0, may hold values from -6 to 6
- line_order: int32 [128], P('groups'), parts along dimension 0, may hold values from 0 to 63, each once
- conv_weight: bfloat16 [3, 3, 3, 256, 128], replicated, may hold values from -0.078125 to 0.078125
- conv_bias: float32 [128], replicated, may hold values from -3 to 3
- blend_table: float32 [4, 8], replicated, may hold values from 0.25 to 4
- blend_ids: int32 [32], P('groups'), parts along dimension 0, may hold values from 0 to 3
Outputs:
- frames: bfloat16 [16, 32, 64, 128], P('groups', None, 'tile'), parts along dimension 0
The draws below stay inside these ranges and needn't reach their ends.
There are 2 independent parts, one for each index of `groups`. The reference program is written for one: setup_inputs(seed, part) draws one part's arguments, and reference() takes and returns one part's arrays. A program takes and returns all parts, laid end to end along the dimension named above; an argument that names none is the same for every part. Nothing has to cross between parts.
Inputs may be any that keep to these rules, and one draw needn't show every extreme that they name: line_order is a permutation of the 64 latent lines.
All inputs are finite; a program needn't handle non-finite values.
Results may differ from the reference program's by a relative error of at most 0.001.
Values may be sent and summed in bfloat16 or wider, within the bound.
No kernel may reach another device: no remote copies, remote signals or barrier semaphores. Data moves between devices by JAX's collectives and lax.ppermute only.
A program may use at most 64 MiB of HBM per device.

```python
import math
import jax
import jax.numpy as jnp
from jax import lax

CI = 256
CO = 128
LT = 4
LH = 16
WD = 2
KINDS = 4
LINES = 64
WIDTH = 32
TILES = 16
TW = 8
OT = 8
OH = 32


def plant(values, key, least, high):
    index_at = [jax.random.randint(jax.random.fold_in(key, axis), (), 0, length) for axis, length in enumerate(values.shape)]
    widest = values.shape.index(max(values.shape))
    beside = index_at[:widest] + [(index_at[widest] + 1) % values.shape[widest]] + index_at[widest + 1:]
    return values.at[tuple(index_at)].set(least).at[tuple(beside)].set(high)


def level_of(rng, shape, split, low, high):
    level = 1.0
    for position, shards_of in split:
        steps = jax.random.uniform(jax.random.fold_in(jax.random.fold_in(rng, 6), position), (shards_of,), jnp.float32, low / len(split), high / len(split))
        level = level * jnp.repeat(jnp.exp(steps), shape[position] // shards_of).reshape((-1,) + (1,) * (len(shape) - 1 - position))
    return level


def noise(stream_key, extent, spread, limit, cuts=(), held_as=jnp.bfloat16):
    entries = jax.random.normal(stream_key, extent, jnp.float32) * spread
    if len(cuts) > 0:
        entries = level_of(stream_key, extent, cuts, -0.22, 0.18) * entries
    return jnp.clip(entries, min=-limit, max=limit).astype(held_as)


def setup_inputs(seed: int = 0, part: int = 0) -> dict:
    key_list = jax.random.split(jax.random.key(seed), 7)
    part_keys = jax.random.split(jax.random.fold_in(key_list[6], part), 7)
    return {
        "latent_rows": noise(part_keys[0], (LINES * WIDTH, CI), 1.0, 6.0, ((0, 16),)),
        "line_order": jax.random.permutation(part_keys[1], LINES).astype(jnp.int32),
        "conv_weight": noise(key_list[2], (3, 3, 3, CI, CO), (27 * CI) ** -0.5, 0.078125),
        "conv_bias": noise(key_list[3], (CO,), 0.5, 3.0, (), jnp.float32),
        "blend_table": jnp.clip(jnp.exp(jax.random.uniform(key_list[4], (KINDS, TW), jnp.float32, math.log(0.25), math.log(4.0))), 0.25, 4.0),
        "blend_ids": plant(jax.random.randint(part_keys[5], (TILES,), 0, KINDS), jax.random.fold_in(part_keys[5], 1), 0, KINDS - 1).astype(jnp.int32),
    }


def upsample(values):
    values = jnp.repeat(values, 2, axis=0)
    values = jnp.repeat(values, 2, axis=1)
    return jnp.repeat(values, 2, axis=2)


def decode_tile(window, conv_weight, conv_bias):
    upsampled = upsample(window).astype(jnp.float32)
    upsampled = jnp.concatenate([upsampled[:1], upsampled[:1], upsampled], axis=0)
    output = lax.conv_general_dilated(upsampled[None], conv_weight.astype(jnp.float32), (1, 1, 1), [(0, 0), (1, 1), (1, 1)], dimension_numbers=("NDHWC", "DHWIO", "NDHWC"), precision=lax.Precision.HIGHEST)[0]
    return jax.nn.silu(output + conv_bias)


def reference(latent_rows, line_order, conv_weight, conv_bias, blend_table, blend_ids):
    token_rows = latent_rows.reshape(LINES, WIDTH, CI)
    inverse = jnp.zeros((LINES,), jnp.int32).at[line_order].set(jnp.arange(LINES, dtype=jnp.int32))
    latent = token_rows[inverse].reshape(LT, LH, WIDTH, CI)
    padded = jnp.pad(latent, ((0, 0), (0, 0), (1, 1), (0, 0)))
    profiles = blend_table[blend_ids]

    def add_tile(totals, tile_at):
        blended, weight_sum = totals
        window = lax.dynamic_slice_in_dim(padded, tile_at * WD, WD + 2, 2)
        decoded = decode_tile(window, conv_weight, conv_bias)
        profile_row = lax.dynamic_index_in_dim(profiles, tile_at, 0, keepdims=False)
        start = (2 * WD * tile_at).astype(jnp.int32)
        current = lax.dynamic_slice_in_dim(blended, start, TW, 2)
        blended = lax.dynamic_update_slice_in_dim(blended, current + profile_row[None, None, :, None] * decoded, start, 2)
        current_sum = lax.dynamic_slice_in_dim(weight_sum, start, TW, 0)
        weight_sum = lax.dynamic_update_slice_in_dim(weight_sum, current_sum + profile_row, start, 0)
        return (blended, weight_sum), None

    start_totals = (jnp.zeros((OT, OH, 2 * WIDTH + 4, CO), jnp.float32), jnp.zeros((2 * WIDTH + 4,), jnp.float32))
    (blended, weight_sum), unused = lax.scan(add_tile, start_totals, jnp.arange(TILES, dtype=jnp.int32))
    return (blended[:, :, 2:-2] / weight_sum[2:-2][None, None, :, None]).astype(jnp.bfloat16)
```

```python
import functools

import jax
import jax.numpy as jnp
from jax import lax
from jax.experimental import pallas as pl
from jax.experimental.pallas import tpu as pltpu
from jax.sharding import PartitionSpec as P

LT = 4
WD = 2
NEIGHBOUR = ((0, 1, None, 2), (1, 1, 2, 2), (1, None, 2, 3))
OWN = ((0, 1, 1, 2), (1, 1, 2, 2), (1, 2, 2, 3))
NONE = 7


def pick(index, values):
    out = jnp.full(index.shape, NONE, jnp.int32)
    for at, value in enumerate(values):
        if value is not None:
            out = jnp.where(index == at, value, out)
    return out


def dot(a, b):
    return jnp.dot(a, b, preferred_element_type=jnp.float32)


def windows_kernel(tiles, x_ref, out_ref):
    rows_in, _ = x_ref.shape
    rows_out = out_ref.shape[0]
    width = tiles * WD
    lines = rows_in // width
    row = lax.broadcasted_iota(jnp.int32, (rows_out, rows_in), 0)
    col = lax.broadcasted_iota(jnp.int32, (rows_out, rows_in), 1)
    span = WD + 2
    tile = row // (lines * span)
    line = (row // span) % lines
    at = tile * WD - 1 + row % span
    hit = (at >= 0) & (at < width) & (line * width + at == col)
    out_ref[...] = dot(hit.astype(jnp.bfloat16), x_ref[...]).astype(jnp.bfloat16)


def select_kernel(tiles, key_ref, ids_ref, table_ref, at_ref, hot_ref, mix_ref):
    rows, cols = hot_ref.shape[1:]
    slot = lax.broadcasted_iota(jnp.int32, (rows, 1), 0)
    key = jnp.broadcast_to(key_ref[...], (rows, cols))
    values = NEIGHBOUR, OWN
    for kw in range(3):
        want = (slot // 8) * 8 + pick(slot % 8, values[0][kw] + values[1][kw])
        hot_ref[kw] = (key == want).astype(jnp.bfloat16)
    at = at_ref[0]
    own = ids_ref[at]
    lower = ids_ref[jnp.maximum(at - 1, 0)]
    upper = ids_ref[jnp.minimum(at + 1, tiles - 1)]
    has_lower = jnp.where(at > 0, 1.0, 0.0)
    has_upper = jnp.where(at < tiles - 1, 1.0, 0.0)
    wide = 2 * WD + 4
    neighbour = [has_lower * table_ref[lower, wide - 2], has_lower * table_ref[lower, wide - 1]]
    neighbour += [has_upper * table_ref[upper, 0], has_upper * table_ref[upper, 1]]
    mine = [table_ref[own, c] for c in range(2, wide - 2)]
    sub = lax.broadcasted_iota(jnp.int32, mix_ref.shape, 0)
    weight = jnp.zeros(mix_ref.shape, jnp.float32)
    total = jnp.ones(mix_ref.shape, jnp.float32)
    for q in range(4):
        weight = jnp.where(sub == q, neighbour[q], weight)
        weight = jnp.where(sub == q + 4, mine[q], weight)
        total = jnp.where(sub % 4 == q, neighbour[q] + mine[q], total)
    mix_ref[...] = weight / total


def decode_kernel(rows_ref, hot_ref, w_ref, bias_ref, mix_ref, out_ref, lhs_ref, part_ref):
    depth = rows_ref.shape[1]
    count = hot_ref.shape[1]
    frame = count // LT
    co = w_ref.shape[1]
    rows = rows_ref[...]
    for kw in range(3):
        lhs_ref[:, kw * depth:(kw + 1) * depth] = dot(hot_ref[kw], rows).astype(jnp.bfloat16)
    taps = [w_ref[k * 3 * depth:(k + 1) * 3 * depth, :] for k in range(9)]
    lhs = lhs_ref[...]
    for k in range(0, 9, 2):
        if k + 1 < 9:
            both = dot(lhs, jnp.concatenate([taps[k], taps[k + 1]], axis=1))
            part_ref[k] = both[:, :co]
            part_ref[k + 1] = both[:, co:]
        else:
            part_ref[k] = dot(lhs, taps[k])
    bias = bias_ref[...]
    mix = jnp.concatenate([mix_ref[...]] * (frame // 8), axis=0)
    low = lax.broadcasted_iota(jnp.int32, (frame, co), 0) % 8 < 4
    zero = jnp.zeros((8, co), jnp.float32)
    before = None
    for t in range(LT):
        now = []
        for kt in range(3):
            p0, p1, p2 = (part_ref[kt * 3 + kh, t * frame:(t + 1) * frame, :] for kh in range(3))
            even = jnp.concatenate([zero, p0[:-8]], axis=0) + (p1 + p2)
            odd = (p0 + p1) + jnp.concatenate([p2[8:], zero], axis=0)
            now.append((even, odd))
        if before is None:
            before = now
        for tp in range(2):
            blended = []
            for hp in range(2):
                middle = before[1][hp] if tp == 0 else now[1][hp]
                value = before[0][hp] + middle + now[2][hp] + bias
                value = value / (1.0 + jnp.exp(-value))
                blended.append(value * mix)
            straight = jnp.where(low, blended[0], blended[1])
            crossed = jnp.where(low, blended[1], blended[0])
            crossed = pltpu.roll(crossed.reshape(frame // 8, 8, co), 4, 1).reshape(frame, co)
            at = (2 * t + tp) * frame
            out_ref[at:at + frame, :] = (straight + crossed).astype(jnp.bfloat16)
        before = now


def vmem():
    return pl.BlockSpec(memory_space=pltpu.VMEM)


def smem():
    return pl.BlockSpec(memory_space=pltpu.SMEM)


def per_device(latent_rows, line_order, conv_weight, conv_bias, blend_table, blend_ids):
    tiles = lax.axis_size("tile")
    rows, depth = latent_rows.shape
    co = conv_weight.shape[-1]
    lines = line_order.shape[0]
    span = WD + 2
    windows = pl.pallas_call(
        functools.partial(windows_kernel, tiles),
        out_shape=jax.ShapeDtypeStruct((lines * span, depth), jnp.bfloat16),
        in_specs=[vmem()],
        out_specs=vmem(),
    )(latent_rows)
    received = lax.all_to_all(windows, "tile", 0, 0, tiled=True)
    key = (line_order[:, None] * 8 + jnp.arange(span, dtype=jnp.int32)[None, :]).reshape(1, lines * span)
    position = lax.axis_index("tile").astype(jnp.int32).reshape(1)
    hot, mix = pl.pallas_call(
        functools.partial(select_kernel, tiles),
        out_shape=(
            jax.ShapeDtypeStruct((3, lines * 8, lines * span), jnp.bfloat16),
            jax.ShapeDtypeStruct((8, co), jnp.float32),
        ),
        in_specs=[vmem(), smem(), smem(), smem()],
        out_specs=(vmem(), vmem()),
    )(key, blend_ids, blend_table, position)
    frame = lines // LT * 8
    out = pl.pallas_call(
        decode_kernel,
        out_shape=jax.ShapeDtypeStruct((2 * LT * frame, co), jnp.bfloat16),
        in_specs=[vmem()] * 5,
        out_specs=vmem(),
        scratch_shapes=[
            pltpu.VMEM((lines * 8, 3 * depth), jnp.bfloat16),
            pltpu.VMEM((9, lines * 8, co), jnp.float32),
        ],
        compiler_params=pltpu.CompilerParams(vmem_limit_bytes=48 * 1024 * 1024),
    )(received, hot, conv_weight.reshape(-1, co), conv_bias.reshape(1, co), mix)
    return out.reshape(2 * LT, lines // LT * 2, 2 * WD, co)


def solution(mesh):
    return jax.shard_map(
        per_device,
        mesh=mesh,
        in_specs=(P(("groups", "tile"), None), P("groups"), P(), P(), P(), P("groups")),
        out_specs=P("groups", None, "tile", None),
        check_vma=False,
    )
```

```python
import functools

import jax
import jax.numpy as jnp
from jax import lax
from jax.experimental import pallas as pl
from jax.experimental.pallas import tpu as pltpu
from jax.sharding import PartitionSpec as P

LT = 4
WD = 2
NEIGHBOUR = ((0, 1, None, 2), (1, 1, 2, 2), (1, None, 2, 3))
OWN = ((0, 1, 1, 2), (1, 1, 2, 2), (1, 2, 2, 3))
NONE = 7


def pick(index, values):
    out = jnp.full(index.shape, NONE, jnp.int32)
    for at, value in enumerate(values):
        if value is not None:
            out = jnp.where(index == at, value, out)
    return out


def dot(a, b):
    return jnp.dot(a, b, preferred_element_type=jnp.float32)


def windows_kernel(tiles, x_hbm, out_ref, x_ref, sem):
    copy = pltpu.make_async_copy(x_hbm, x_ref, sem)
    copy.start()
    rows_in, _ = x_ref.shape
    rows_out = out_ref.shape[0]
    width = tiles * WD
    span = WD + 2
    per_tile = rows_in // width * span
    row = lax.broadcasted_iota(jnp.int32, (rows_out, 1), 0)
    tile = lax.div(row, per_tile)
    line = lax.div(lax.rem(row, per_tile), span)
    at = tile * WD - 1 + lax.rem(row, span)
    want = jnp.where((at >= 0) & (at < width), line * width + at, -1)
    col = lax.broadcasted_iota(jnp.int32, (rows_out, rows_in), 1)
    hot = (want == col).astype(jnp.bfloat16)
    copy.wait()
    out_ref[...] = dot(hot, x_ref[...]).astype(jnp.bfloat16)


def select_kernel(tiles, order_ref, ids_ref, table_ref, at_ref, w_hbm, bias_in, hot_ref, mix_ref, w_ref, bias_ref, sem):
    copy = pltpu.make_async_copy(w_hbm, w_ref, sem)
    copy.start()
    bias_ref[...] = bias_in[...]
    rows, cols = hot_ref.shape[1:]
    lines = order_ref.shape[1]
    span = WD + 2
    spread = lax.broadcasted_iota(jnp.int32, (lines, cols), 0) == lax.div(
        lax.broadcasted_iota(jnp.int32, (lines, cols), 1), span
    )
    order = jnp.broadcast_to(order_ref[...].astype(jnp.float32), (8, lines))
    order = jnp.dot(order, spread.astype(jnp.float32), precision=lax.Precision.HIGHEST)[:1]
    column = lax.rem(lax.broadcasted_iota(jnp.int32, (1, cols), 1), span)
    key = jnp.broadcast_to(order.astype(jnp.int32) * 8 + column, (rows, cols))
    slot = lax.broadcasted_iota(jnp.int32, (rows, 1), 0)
    inside = lax.rem(slot, 8)
    for kw in range(3):
        want = slot - inside + pick(inside, NEIGHBOUR[kw] + OWN[kw])
        hot_ref[kw] = (key == want).astype(jnp.bfloat16)
    at = at_ref[0]
    own = ids_ref[at]
    lower = ids_ref[jnp.maximum(at - 1, 0)]
    upper = ids_ref[jnp.minimum(at + 1, tiles - 1)]
    has_lower = jnp.where(at > 0, 1.0, 0.0)
    has_upper = jnp.where(at < tiles - 1, 1.0, 0.0)
    wide = 2 * WD + 4
    neighbour = [has_lower * table_ref[lower, wide - 2], has_lower * table_ref[lower, wide - 1]]
    neighbour += [has_upper * table_ref[upper, 0], has_upper * table_ref[upper, 1]]
    mine = [table_ref[own, c] for c in range(2, wide - 2)]
    sub = lax.broadcasted_iota(jnp.int32, mix_ref.shape, 0)
    weight = jnp.zeros(mix_ref.shape, jnp.float32)
    total = jnp.ones(mix_ref.shape, jnp.float32)
    for q in range(4):
        weight = jnp.where(sub == q, neighbour[q], weight)
        weight = jnp.where(sub == q + 4, mine[q], weight)
        total = jnp.where(lax.rem(sub, 4) == q, neighbour[q] + mine[q], total)
    mix_ref[...] = weight / total
    copy.wait()


def decode_kernel(rows_ref, hot_ref, w_ref, bias_ref, mix_ref, out_ref, lhs_ref, part_ref):
    depth = rows_ref.shape[1]
    count = hot_ref.shape[1]
    frame = count // LT
    co = w_ref.shape[1]
    rows = rows_ref[...]
    for kw in range(3):
        lhs_ref[:, kw * depth:(kw + 1) * depth] = dot(hot_ref[kw], rows).astype(jnp.bfloat16)
    taps = [w_ref[k * 3 * depth:(k + 1) * 3 * depth, :] for k in range(9)]
    lhs = lhs_ref[...]
    for k in range(0, 9, 2):
        if k + 1 < 9:
            both = dot(lhs, jnp.concatenate([taps[k], taps[k + 1]], axis=1))
            part_ref[k] = both[:, :co]
            part_ref[k + 1] = both[:, co:]
        else:
            part_ref[k] = dot(lhs, taps[k])
    bias = bias_ref[...]
    mix = jnp.concatenate([mix_ref[...]] * (frame // 8), axis=0)
    low = lax.broadcasted_iota(jnp.int32, (frame, co), 0) % 8 < 4
    zero = jnp.zeros((8, co), jnp.float32)
    before = None
    for t in range(LT):
        now = []
        for kt in range(3):
            p0, p1, p2 = (part_ref[kt * 3 + kh, t * frame:(t + 1) * frame, :] for kh in range(3))
            even = jnp.concatenate([zero, p0[:-8]], axis=0) + (p1 + p2)
            odd = (p0 + p1) + jnp.concatenate([p2[8:], zero], axis=0)
            now.append((even, odd))
        if before is None:
            before = now
        for tp in range(2):
            blended = []
            for hp in range(2):
                middle = before[1][hp] if tp == 0 else now[1][hp]
                value = before[0][hp] + middle + now[2][hp] + bias
                value = value / (1.0 + jnp.exp(-value))
                blended.append(value * mix)
            straight = jnp.where(low, blended[0], blended[1])
            crossed = jnp.where(low, blended[1], blended[0])
            crossed = pltpu.roll(crossed.reshape(frame // 8, 8, co), 4, 1).reshape(frame, co)
            at = (2 * t + tp) * frame
            out_ref[at:at + frame, :] = (straight + crossed).astype(jnp.bfloat16)
        before = now


def vmem():
    return pl.BlockSpec(memory_space=pltpu.VMEM)


def smem():
    return pl.BlockSpec(memory_space=pltpu.SMEM)


def hbm():
    return pl.BlockSpec(memory_space=pl.ANY)


def held(value):
    return pltpu.with_memory_space_constraint(value, pltpu.VMEM)


def per_device(latent_rows, line_order, conv_weight, conv_bias, blend_table, blend_ids):
    tiles = lax.axis_size("tile")
    rows, depth = latent_rows.shape
    co = conv_weight.shape[-1]
    lines = line_order.shape[0]
    span = WD + 2
    weights = conv_weight.reshape(-1, co)
    windows = pl.pallas_call(
        functools.partial(windows_kernel, tiles),
        out_shape=pltpu.VMEM((lines * span, depth), jnp.bfloat16),
        in_specs=[hbm()],
        out_specs=vmem(),
        scratch_shapes=[pltpu.VMEM((rows, depth), jnp.bfloat16), pltpu.SemaphoreType.DMA],
    )(latent_rows)
    received = lax.all_to_all(windows, "tile", 0, 0, tiled=True)
    position = lax.axis_index("tile").astype(jnp.int32).reshape(1)
    hot, mix, weights, bias = pl.pallas_call(
        functools.partial(select_kernel, tiles),
        out_shape=(
            pltpu.VMEM((3, lines * 8, lines * span), jnp.bfloat16),
            pltpu.VMEM((8, co), jnp.float32),
            pltpu.VMEM(weights.shape, weights.dtype),
            pltpu.VMEM((1, co), jnp.float32),
        ),
        in_specs=[vmem(), smem(), smem(), smem(), hbm(), vmem()],
        out_specs=(vmem(),) * 4,
        scratch_shapes=[pltpu.SemaphoreType.DMA],
    )(line_order.reshape(1, -1), blend_ids, blend_table, position, weights, conv_bias.reshape(1, co))
    frame = lines // LT * 8
    out = pl.pallas_call(
        decode_kernel,
        out_shape=jax.ShapeDtypeStruct((2 * LT * frame, co), jnp.bfloat16),
        in_specs=[vmem()] * 5,
        out_specs=vmem(),
        scratch_shapes=[
            pltpu.VMEM((lines * 8, 3 * depth), jnp.bfloat16),
            pltpu.VMEM((9, lines * 8, co), jnp.float32),
        ],
        compiler_params=pltpu.CompilerParams(vmem_limit_bytes=48 * 1024 * 1024),
    )(held(received), held(hot), held(weights), held(bias), held(mix))
    return out.reshape(2 * LT, lines // LT * 2, 2 * WD, co)


def solution(mesh):
    return jax.shard_map(
        per_device,
        mesh=mesh,
        in_specs=(P(("groups", "tile"), None), P("groups"), P(), P(), P(), P("groups")),
        out_specs=P("groups", None, "tile", None),
        check_vma=False,
    )
```

```python
import functools

import jax
import jax.numpy as jnp
from jax import lax
from jax.experimental import pallas as pl
from jax.experimental.pallas import tpu as pltpu
from jax.sharding import PartitionSpec as P

LT = 4
WD = 2
NEIGHBOUR = ((0, 1, None, 2), (1, 1, 2, 2), (1, None, 2, 3))
OWN = ((0, 1, 1, 2), (1, 1, 2, 2), (1, 2, 2, 3))
NONE = 7


def tile_of(place, tiles):
    return (tiles + 3 * tiles // 4 - 1 - place) % tiles


def pick(index, values):
    out = jnp.full(index.shape, NONE, jnp.int32)
    for at, value in enumerate(values):
        if value is not None:
            out = jnp.where(index == at, value, out)
    return out


def dot(a, b):
    return jnp.dot(a, b, preferred_element_type=jnp.float32)


def windows_kernel(tiles, x_hbm, out_ref, x_ref, sem):
    copy = pltpu.make_async_copy(x_hbm, x_ref, sem)
    copy.start()
    rows_in, _ = x_ref.shape
    rows_out = out_ref.shape[0]
    width = tiles * WD
    span = WD + 2
    per_tile = rows_in // width * span
    row = lax.broadcasted_iota(jnp.int32, (rows_out, 1), 0)
    tile = tile_of(lax.div(row, per_tile), tiles)
    line = lax.div(lax.rem(row, per_tile), span)
    at = tile * WD - 1 + lax.rem(row, span)
    want = jnp.where((at >= 0) & (at < width), line * width + at, -1)
    col = lax.broadcasted_iota(jnp.int32, (rows_out, rows_in), 1)
    hot = (want == col).astype(jnp.bfloat16)
    copy.wait()
    out_ref[...] = dot(hot, x_ref[...]).astype(jnp.bfloat16)


def select_kernel(tiles, order_ref, ids_ref, table_ref, at_ref, w_hbm, bias_in, hot_ref, mix_ref, w_ref, bias_ref, sem):
    copy = pltpu.make_async_copy(w_hbm, w_ref, sem)
    copy.start()
    bias_ref[...] = bias_in[...]
    rows, cols = hot_ref.shape[1:]
    lines = order_ref.shape[1]
    span = WD + 2
    line_at = lax.div(lax.broadcasted_iota(jnp.int32, (lines, cols), 1), span)
    per_tile = lines // tiles
    line_at = tile_of(lax.div(line_at, per_tile), tiles) * per_tile + lax.rem(line_at, per_tile)
    spread = lax.broadcasted_iota(jnp.int32, (lines, cols), 0) == line_at
    order = jnp.broadcast_to(order_ref[...].astype(jnp.float32), (8, lines))
    order = jnp.dot(order, spread.astype(jnp.float32), precision=lax.Precision.HIGHEST)[:1]
    column = lax.rem(lax.broadcasted_iota(jnp.int32, (1, cols), 1), span)
    key = jnp.broadcast_to(order.astype(jnp.int32) * 8 + column, (rows, cols))
    slot = lax.broadcasted_iota(jnp.int32, (rows, 1), 0)
    inside = lax.rem(slot, 8)
    for kw in range(3):
        want = slot - inside + pick(inside, NEIGHBOUR[kw] + OWN[kw])
        hot_ref[kw] = (key == want).astype(jnp.bfloat16)
    at = at_ref[0]
    own = ids_ref[at]
    lower = ids_ref[jnp.maximum(at - 1, 0)]
    upper = ids_ref[jnp.minimum(at + 1, tiles - 1)]
    has_lower = jnp.where(at > 0, 1.0, 0.0)
    has_upper = jnp.where(at < tiles - 1, 1.0, 0.0)
    wide = 2 * WD + 4
    neighbour = [has_lower * table_ref[lower, wide - 2], has_lower * table_ref[lower, wide - 1]]
    neighbour += [has_upper * table_ref[upper, 0], has_upper * table_ref[upper, 1]]
    mine = [table_ref[own, c] for c in range(2, wide - 2)]
    sub = lax.broadcasted_iota(jnp.int32, mix_ref.shape, 0)
    weight = jnp.zeros(mix_ref.shape, jnp.float32)
    total = jnp.ones(mix_ref.shape, jnp.float32)
    for q in range(4):
        weight = jnp.where(sub == q, neighbour[q], weight)
        weight = jnp.where(sub == q + 4, mine[q], weight)
        total = jnp.where(lax.rem(sub, 4) == q, neighbour[q] + mine[q], total)
    mix_ref[...] = weight / total
    copy.wait()


def decode_kernel(rows_ref, hot_ref, w_ref, bias_ref, mix_ref, out_ref, lhs_ref, part_ref):
    depth = rows_ref.shape[1]
    count = hot_ref.shape[1]
    frame = count // LT
    co = w_ref.shape[1]
    rows = rows_ref[...]
    for kw in range(3):
        lhs_ref[:, kw * depth:(kw + 1) * depth] = dot(hot_ref[kw], rows).astype(jnp.bfloat16)
    taps = [w_ref[k * 3 * depth:(k + 1) * 3 * depth, :] for k in range(9)]
    lhs = lhs_ref[...]
    for k in range(0, 9, 2):
        if k + 1 < 9:
            both = dot(lhs, jnp.concatenate([taps[k], taps[k + 1]], axis=1))
            part_ref[k] = both[:, :co]
            part_ref[k + 1] = both[:, co:]
        else:
            part_ref[k] = dot(lhs, taps[k])
    bias = bias_ref[...]
    mix = jnp.concatenate([mix_ref[...]] * (frame // 8), axis=0)
    low = lax.broadcasted_iota(jnp.int32, (frame, co), 0) % 8 < 4
    zero = jnp.zeros((8, co), jnp.float32)
    before = None
    for t in range(LT):
        now = []
        for kt in range(3):
            p0, p1, p2 = (part_ref[kt * 3 + kh, t * frame:(t + 1) * frame, :] for kh in range(3))
            even = jnp.concatenate([zero, p0[:-8]], axis=0) + (p1 + p2)
            odd = (p0 + p1) + jnp.concatenate([p2[8:], zero], axis=0)
            now.append((even, odd))
        if before is None:
            before = now
        for tp in range(2):
            blended = []
            for hp in range(2):
                middle = before[1][hp] if tp == 0 else now[1][hp]
                value = before[0][hp] + middle + now[2][hp] + bias
                value = value / (1.0 + jnp.exp(-value))
                blended.append(value * mix)
            straight = jnp.where(low, blended[0], blended[1])
            crossed = jnp.where(low, blended[1], blended[0])
            crossed = pltpu.roll(crossed.reshape(frame // 8, 8, co), 4, 1).reshape(frame, co)
            at = (2 * t + tp) * frame
            out_ref[at:at + frame, :] = (straight + crossed).astype(jnp.bfloat16)
        before = now


def vmem():
    return pl.BlockSpec(memory_space=pltpu.VMEM)


def smem():
    return pl.BlockSpec(memory_space=pltpu.SMEM)


def hbm():
    return pl.BlockSpec(memory_space=pl.ANY)


def held(value):
    return pltpu.with_memory_space_constraint(value, pltpu.VMEM)


def per_device(latent_rows, line_order, conv_weight, conv_bias, blend_table, blend_ids):
    tiles = lax.axis_size("tile")
    rows, depth = latent_rows.shape
    co = conv_weight.shape[-1]
    lines = line_order.shape[0]
    span = WD + 2
    weights = conv_weight.reshape(-1, co)
    windows = pl.pallas_call(
        functools.partial(windows_kernel, tiles),
        out_shape=pltpu.VMEM((lines * span, depth), jnp.bfloat16),
        in_specs=[hbm()],
        out_specs=vmem(),
        scratch_shapes=[pltpu.VMEM((rows, depth), jnp.bfloat16), pltpu.SemaphoreType.DMA],
    )(latent_rows)
    order = [tile_of(place, tiles) for place in range(tiles)]
    received = lax.all_to_all(windows, "tile", 0, 0, axis_index_groups=[order], tiled=True)
    position = lax.axis_index("tile").astype(jnp.int32).reshape(1)
    hot, mix, weights, bias = pl.pallas_call(
        functools.partial(select_kernel, tiles),
        out_shape=(
            pltpu.VMEM((3, lines * 8, lines * span), jnp.bfloat16),
            pltpu.VMEM((8, co), jnp.float32),
            pltpu.VMEM(weights.shape, weights.dtype),
            pltpu.VMEM((1, co), jnp.float32),
        ),
        in_specs=[vmem(), smem(), smem(), smem(), hbm(), vmem()],
        out_specs=(vmem(),) * 4,
        scratch_shapes=[pltpu.SemaphoreType.DMA],
    )(line_order.reshape(1, -1), blend_ids, blend_table, position, weights, conv_bias.reshape(1, co))
    frame = lines // LT * 8
    out = pl.pallas_call(
        decode_kernel,
        out_shape=jax.ShapeDtypeStruct((2 * LT * frame, co), jnp.bfloat16),
        in_specs=[vmem()] * 5,
        out_specs=vmem(),
        scratch_shapes=[
            pltpu.VMEM((lines * 8, 3 * depth), jnp.bfloat16),
            pltpu.VMEM((9, lines * 8, co), jnp.float32),
        ],
        compiler_params=pltpu.CompilerParams(vmem_limit_bytes=48 * 1024 * 1024),
    )(held(received), held(hot), held(weights), held(bias), held(mix))
    return out.reshape(2 * LT, lines // LT * 2, 2 * WD, co)


def solution(mesh):
    return jax.shard_map(
        per_device,
        mesh=mesh,
        in_specs=(P(("groups", "tile"), None), P("groups"), P(), P(), P(), P("groups")),
        out_specs=P("groups", None, "tile", None),
        check_vma=False,
    )
```

```python
import functools

import jax
import jax.numpy as jnp
from jax import lax
from jax.experimental import pallas as pl
from jax.experimental.pallas import tpu as pltpu
from jax.sharding import PartitionSpec as P

LT = 4
WD = 2
NEIGHBOUR = ((0, 1, None, 2), (1, 1, 2, 2), (1, None, 2, 3))
OWN = ((0, 1, 1, 2), (1, 1, 2, 2), (1, 2, 2, 3))
NONE = 7


def tile_of(place, tiles):
    return (tiles + 3 * tiles // 4 - 1 - place) % tiles


def pick(index, values):
    out = jnp.full(index.shape, NONE, jnp.int32)
    for at, value in enumerate(values):
        if value is not None:
            out = jnp.where(index == at, value, out)
    return out


def dot(a, b):
    return jnp.dot(a, b, preferred_element_type=jnp.float32)


def windows_hot(tiles, rows_in, rows_out):
    width = tiles * WD
    span = WD + 2
    per_tile = rows_in // width * span
    row = lax.broadcasted_iota(jnp.int32, (rows_out, 1), 0)
    tile = tile_of(lax.div(row, per_tile), tiles)
    line = lax.div(lax.rem(row, per_tile), span)
    at = tile * WD - 1 + lax.rem(row, span)
    want = jnp.where((at >= 0) & (at < width), line * width + at, -1)
    col = lax.broadcasted_iota(jnp.int32, (rows_out, rows_in), 1)
    return (want == col).astype(jnp.bfloat16)


def line_key(tiles, order, cols):
    lines = order.shape[1]
    span = WD + 2
    per_tile = lines // tiles
    line_at = lax.div(lax.broadcasted_iota(jnp.int32, (lines, cols), 1), span)
    line_at = tile_of(lax.div(line_at, per_tile), tiles) * per_tile + lax.rem(line_at, per_tile)
    spread = lax.broadcasted_iota(jnp.int32, (lines, cols), 0) == line_at
    order = jnp.broadcast_to(order.astype(jnp.float32), (8, lines))
    order = jnp.dot(order, spread.astype(jnp.float32), precision=lax.Precision.HIGHEST)[:1]
    column = lax.rem(lax.broadcasted_iota(jnp.int32, (1, cols), 1), span)
    return order.astype(jnp.int32) * 8 + column


def blend_mix(tiles, at, ids_ref, table_ref, shape):
    own = ids_ref[at]
    lower = ids_ref[jnp.maximum(at - 1, 0)]
    upper = ids_ref[jnp.minimum(at + 1, tiles - 1)]
    has_lower = jnp.where(at > 0, 1.0, 0.0)
    has_upper = jnp.where(at < tiles - 1, 1.0, 0.0)
    wide = 2 * WD + 4
    neighbour = [has_lower * table_ref[lower, wide - 2], has_lower * table_ref[lower, wide - 1]]
    neighbour += [has_upper * table_ref[upper, 0], has_upper * table_ref[upper, 1]]
    mine = [table_ref[own, c] for c in range(2, wide - 2)]
    sub = lax.broadcasted_iota(jnp.int32, shape, 0)
    weight = jnp.zeros(shape, jnp.float32)
    total = jnp.ones(shape, jnp.float32)
    for q in range(4):
        weight = jnp.where(sub == q, neighbour[q], weight)
        weight = jnp.where(sub == q + 4, mine[q], weight)
        total = jnp.where(lax.rem(sub, 4) == q, neighbour[q] + mine[q], total)
    return weight / total


def prepare_kernel(
    tiles, x_hbm, order_hbm, ids_hbm, table_hbm, bias_hbm, at_ref,
    x_ref, take_ref, hot_ref, mix_ref, bias_ref, order_ref, ids_ref, table_ref, sems,
):
    moves = [
        (order_hbm, order_ref), (x_hbm, x_ref), (ids_hbm, ids_ref), (table_hbm, table_ref), (bias_hbm, bias_ref),
    ]
    copies = [pltpu.make_async_copy(a, b, sems.at[n]) for n, (a, b) in enumerate(moves)]
    for copy in copies:
        copy.start()
    take_ref[...] = windows_hot(tiles, *take_ref.shape[::-1])
    rows, cols = hot_ref.shape[1:]
    slot = lax.broadcasted_iota(jnp.int32, (rows, 1), 0)
    inside = lax.rem(slot, 8)
    wants = [slot - inside + pick(inside, NEIGHBOUR[kw] + OWN[kw]) for kw in range(3)]
    copies[0].wait()
    key = jnp.broadcast_to(line_key(tiles, order_ref[...], cols), (rows, cols))
    for kw in range(3):
        hot_ref[kw] = (key == wants[kw]).astype(jnp.bfloat16)
    for copy in copies[2:]:
        copy.wait()
    mix_ref[...] = blend_mix(tiles, at_ref[0], ids_ref, table_ref, mix_ref.shape)
    copies[1].wait()


def windows_kernel(x_ref, take_ref, send_ref):
    send_ref[...] = dot(take_ref[...], x_ref[...]).astype(jnp.bfloat16)


def decode_kernel(rows_ref, hot_ref, w_ref, bias_ref, mix_ref, out_hbm, lhs_ref, part_ref, out_ref, sems):
    depth = rows_ref.shape[1]
    count = hot_ref.shape[1]
    frame = count // LT
    co = w_ref.shape[1]
    tap = 3 * depth
    rows = rows_ref[...]
    for kw in range(3):
        lhs_ref[:, kw * depth:(kw + 1) * depth] = dot(hot_ref[kw], rows).astype(jnp.bfloat16)
    def weights(k):
        return w_ref[k * tap:(k + 1) * tap, :]

    bias = bias_ref[...]
    mix = jnp.concatenate([mix_ref[...]] * (frame // 8), axis=0)
    low = lax.broadcasted_iota(jnp.int32, (frame, co), 0) % 8 < 4
    zero = jnp.zeros((8, co), jnp.float32)
    before = None
    copies = []
    group = count // 4
    for t in range(LT):
        if t * frame % group == 0:
            here = slice(t * frame, t * frame + group)
            lhs = lhs_ref[here, :]
            for k in range(0, 9, 2):
                if k + 1 < 9:
                    both = dot(lhs, jnp.concatenate([weights(k), weights(k + 1)], axis=1))
                    part_ref[k, here] = both[:, :co]
                    part_ref[k + 1, here] = both[:, co:]
                else:
                    part_ref[k, here] = dot(lhs, weights(k))
        now = []
        for kt in range(3):
            p0, p1, p2 = (part_ref[kt * 3 + kh, t * frame:(t + 1) * frame, :] for kh in range(3))
            even = jnp.concatenate([zero, p0[:-8]], axis=0) + (p1 + p2)
            odd = (p0 + p1) + jnp.concatenate([p2[8:], zero], axis=0)
            now.append((even, odd))
        if before is None:
            before = now
        for tp in range(2):
            blended = []
            for hp in range(2):
                middle = before[1][hp] if tp == 0 else now[1][hp]
                value = before[0][hp] + middle + now[2][hp] + bias
                value = value / (1.0 + jnp.exp(-value))
                blended.append(value * mix)
            straight = jnp.where(low, blended[0], blended[1])
            crossed = jnp.where(low, blended[1], blended[0])
            crossed = pltpu.roll(crossed.reshape(frame // 8, 8, co), 4, 1).reshape(frame, co)
            at = (2 * t + tp) * frame
            out_ref[at:at + frame, :] = (straight + crossed).astype(jnp.bfloat16)
            frames = pl.ds(at, frame)
            copies.append(pltpu.make_async_copy(out_ref.at[frames], out_hbm.at[frames], sems.at[2 * t + tp]))
            copies[-1].start()
        before = now
    for copy in copies:
        copy.wait()


def vmem():
    return pl.BlockSpec(memory_space=pltpu.VMEM)


def smem():
    return pl.BlockSpec(memory_space=pltpu.SMEM)


def hbm():
    return pl.BlockSpec(memory_space=pltpu.HBM)


def outside(value):
    return pltpu.with_memory_space_constraint(value, pltpu.HBM)


def held(value):
    return pltpu.with_memory_space_constraint(value, pltpu.VMEM)


def per_device(latent_rows, line_order, conv_weight, conv_bias, blend_table, blend_ids):
    tiles = lax.axis_size("tile")
    rows, depth = latent_rows.shape
    co = conv_weight.shape[-1]
    lines = line_order.shape[0]
    span = WD + 2
    weights = conv_weight.reshape(-1, co)
    order = [tile_of(place, tiles) for place in range(tiles)]
    position = lax.axis_index("tile").astype(jnp.int32).reshape(1)
    x, take, hot, mix, bias = pl.pallas_call(
        functools.partial(prepare_kernel, tiles),
        out_shape=(
            pltpu.VMEM((rows, depth), jnp.bfloat16),
            pltpu.VMEM((lines * span, rows), jnp.bfloat16),
            pltpu.VMEM((3, lines * 8, lines * span), jnp.bfloat16),
            pltpu.VMEM((8, co), jnp.float32),
            pltpu.VMEM((1, co), jnp.float32),
        ),
        in_specs=[hbm()] * 5 + [smem()],
        out_specs=(vmem(),) * 5,
        scratch_shapes=[
            pltpu.VMEM((1, lines), jnp.int32),
            pltpu.SMEM(blend_ids.shape, jnp.int32),
            pltpu.SMEM(blend_table.shape, jnp.float32),
            pltpu.SemaphoreType.DMA((5,)),
        ],
    )(
        *map(outside, (latent_rows, line_order.reshape(1, -1), blend_ids, blend_table, conv_bias.reshape(1, co))),
        position,
    )
    send = pl.pallas_call(
        windows_kernel,
        out_shape=pltpu.VMEM((lines * span, depth), jnp.bfloat16),
        in_specs=[vmem(), vmem()],
        out_specs=vmem(),
        cost_estimate=pl.CostEstimate(flops=10**10, bytes_accessed=10**7, transcendentals=0),
    )(held(x), held(take))
    received = lax.all_to_all(send, "tile", 0, 0, axis_index_groups=[order], tiled=True)
    frame = lines // LT * 8
    out = pl.pallas_call(
        decode_kernel,
        out_shape=jax.ShapeDtypeStruct((2 * LT * frame, co), jnp.bfloat16),
        in_specs=[vmem()] * 5,
        out_specs=hbm(),
        scratch_shapes=[
            pltpu.VMEM((lines * 8, 3 * depth), jnp.bfloat16),
            pltpu.VMEM((9, lines * 8, co), jnp.float32),
            pltpu.VMEM((2 * LT * frame, co), jnp.bfloat16),
            pltpu.SemaphoreType.DMA((2 * LT,)),
        ],
        compiler_params=pltpu.CompilerParams(vmem_limit_bytes=48 * 1024 * 1024),
    )(held(received), held(hot), weights, held(bias), held(mix))
    return out.reshape(2 * LT, lines // LT * 2, 2 * WD, co)


def solution(mesh):
    return jax.shard_map(
        per_device,
        mesh=mesh,
        in_specs=(P(("groups", "tile"), None), P("groups"), P(), P(), P(), P("groups")),
        out_specs=P("groups", None, "tile", None),
        check_vma=False,
    )
```

```python
import functools

import jax
import jax.numpy as jnp
from jax import lax
from jax.experimental import pallas as pl
from jax.experimental.pallas import tpu as pltpu
from jax.sharding import PartitionSpec as P

LT = 4
WD = 2
OWN = ((0, 1, 1, 2), (1, 1, 2, 2), (1, 2, 2, 3))
NEIGHBOUR = ((None, 1, None, None), (None, 1, 2, None), (None, None, 2, None))
NONE = 7
PACKED = ((1, 0, 2), (0, 0, 1), (0, 0, 2), (1, 1, 1), (1, 1, 2), (0, 1, 1), (0, 1, 2), (1, 0, 1))


def tile_of(place, tiles):
    return (tiles + 3 * tiles // 4 - 1 - place) % tiles


def pick(index, values):
    out = jnp.full(index.shape, NONE, jnp.int32)
    for at, value in enumerate(values):
        if value is not None:
            out = jnp.where(index == at, value, out)
    return out


def dot(a, b):
    return jnp.dot(a, b, preferred_element_type=jnp.float32)


def windows_hot(tiles, rows_in, rows_out):
    width = tiles * WD
    span = WD + 2
    per_tile = rows_in // width * span
    row = lax.broadcasted_iota(jnp.int32, (rows_out, 1), 0)
    tile = tile_of(lax.div(row, per_tile), tiles)
    line = lax.div(lax.rem(row, per_tile), span)
    at = tile * WD - 1 + lax.rem(row, span)
    want = jnp.where((at >= 0) & (at < width), line * width + at, -1)
    col = lax.broadcasted_iota(jnp.int32, (rows_out, rows_in), 1)
    return (want == col).astype(jnp.bfloat16)


def line_key(tiles, order, cols):
    lines = order.shape[1]
    span = WD + 2
    per_tile = lines // tiles
    line_at = lax.div(lax.broadcasted_iota(jnp.int32, (lines, cols), 1), span)
    line_at = tile_of(lax.div(line_at, per_tile), tiles) * per_tile + lax.rem(line_at, per_tile)
    spread = lax.broadcasted_iota(jnp.int32, (lines, cols), 0) == line_at
    order = jnp.broadcast_to(order.astype(jnp.float32), (8, lines))
    order = jnp.dot(order, spread.astype(jnp.float32), precision=lax.Precision.HIGHEST)[:1]
    column = lax.rem(lax.broadcasted_iota(jnp.int32, (1, cols), 1), span)
    return order.astype(jnp.int32) * 8 + column


def blend_mix(tiles, at, ids_ref, table_ref, shape):
    own = ids_ref[at]
    lower = ids_ref[jnp.maximum(at - 1, 0)]
    upper = ids_ref[jnp.minimum(at + 1, tiles - 1)]
    has_lower = jnp.where(at > 0, 1.0, 0.0)
    has_upper = jnp.where(at < tiles - 1, 1.0, 0.0)
    wide = 2 * WD + 4
    neighbour = [has_lower * table_ref[lower, wide - 2], has_lower * table_ref[lower, wide - 1]]
    neighbour += [has_upper * table_ref[upper, 0], has_upper * table_ref[upper, 1]]
    mine = [table_ref[own, c] for c in range(2, wide - 2)]
    sub = lax.rem(lax.broadcasted_iota(jnp.int32, shape, 0), 4)
    other = jnp.zeros(shape, jnp.float32)
    same = jnp.zeros(shape, jnp.float32)
    for q in range(4):
        other = jnp.where(sub == q, neighbour[q], other)
        same = jnp.where(sub == q, mine[q], same)
    total = same + other
    differs = (sub == 1) | (sub == 2)
    return jnp.where(differs, same, total) / total, jnp.where(differs, other, 0.0) / total


def wanted_keys(rows, lines):
    height = lines // LT
    half = height // 2
    row = lax.broadcasted_iota(jnp.int32, (rows, 1), 0)
    sub = lax.rem(row, 8)
    group = lax.div(row, 8)
    packed = LT // 2 * half
    own = group >= packed
    group = jnp.where(own, group - packed, group)
    later, lower, column = (pick(sub, [entry[n] for entry in PACKED]) for n in range(3))
    frame = lax.div(group, half) + jnp.where(own, 0, later * (LT // 2))
    at = lax.rem(group, half) + half * jnp.where(own, lax.div(sub, 4), lower)
    column = jnp.where(own, lax.rem(sub, 4), column)
    line = (frame * height + at) * 8
    return [line + jnp.where(own, pick(column, OWN[kw]), pick(column, NEIGHBOUR[kw])) for kw in range(3)]


def prepare_kernel(
    tiles, x_hbm, order_hbm, ids_hbm, table_hbm, bias_hbm, at_ref,
    x_ref, take_ref, hot_ref, mix_ref, bias_ref, order_ref, ids_ref, table_ref, sems,
):
    moves = [
        (order_hbm, order_ref), (x_hbm, x_ref), (ids_hbm, ids_ref), (table_hbm, table_ref), (bias_hbm, bias_ref),
    ]
    copies = [pltpu.make_async_copy(a, b, sems.at[n]) for n, (a, b) in enumerate(moves)]
    for copy in copies:
        copy.start()
    take_ref[...] = windows_hot(tiles, *take_ref.shape[::-1])
    rows, cols = hot_ref.shape[1:]
    wants = wanted_keys(rows, order_ref.shape[1])
    copies[0].wait()
    key = jnp.broadcast_to(line_key(tiles, order_ref[...], cols), (rows, cols))
    for kw in range(3):
        hot_ref[kw] = (key == wants[kw]).astype(jnp.bfloat16)
    for copy in copies[2:]:
        copy.wait()
    mix_ref[0], mix_ref[1] = blend_mix(tiles, at_ref[0], ids_ref, table_ref, mix_ref.shape[1:])
    copies[1].wait()


def windows_kernel(x_ref, take_ref, send_ref):
    send_ref[...] = dot(take_ref[...], x_ref[...]).astype(jnp.bfloat16)


def turn(value, by):
    shape = value.shape
    return pltpu.roll(value.reshape(shape[0] // 8, 8, shape[1]), by, 1).reshape(shape)


def silu(value):
    return 0.5 * value * (1.0 + jnp.tanh(0.5 * value))


def decode_kernel(rows_ref, hot_ref, w_ref, bias_ref, mix_ref, out_hbm, part_ref, out_ref, sems):
    depth = rows_ref.shape[1]
    count = hot_ref.shape[1]
    co = w_ref.shape[1]
    tap = 3 * depth
    frame = count // (LT + LT // 2)
    groups = frame // 8
    rows = rows_ref[...]
    bias = bias_ref[...]
    sub = lax.rem(lax.broadcasted_iota(jnp.int32, (frame, co), 0), 8)
    low = sub < 4
    upper_own = low[:8]
    upper_packed = (sub[:8] < 3) | (sub[:8] == 7)
    earlier = lax.rem(sub, 4)
    earlier = (earlier == 1) | (earlier == 2)
    own_weight = jnp.concatenate([mix_ref[0]] * groups, axis=0)
    other_weight = jnp.concatenate([mix_ref[1]] * groups, axis=0)

    def multiply(at, size):
        here = slice(at, at + size)
        lhs = jnp.concatenate([dot(hot_ref[kw, here], rows).astype(jnp.bfloat16) for kw in range(3)], axis=1)
        for k in range(0, 9, 2):
            if k + 1 < 9:
                pair = [w_ref[n * tap:(n + 1) * tap, :] for n in (k, k + 1)]
                both = dot(lhs, jnp.concatenate(pair, axis=1))
                part_ref[k, here] = both[:, :co]
                part_ref[k + 1, here] = both[:, co:]
            else:
                part_ref[k, here] = dot(lhs, w_ref[k * tap:(k + 1) * tap, :])

    def over_rows(at, upper):
        sums = []
        for kt in range(3):
            p0, p1, p2 = (part_ref[kt * 3 + kh, at:at + frame, :] for kh in range(3))
            above = jnp.concatenate([jnp.where(upper, 0.0, turn(p0[-8:], 4)), p0[:-8]], axis=0)
            below = jnp.concatenate([p2[8:], jnp.where(upper, turn(p2[:8], 4), 0.0)], axis=0)
            sums.append((above + (p1 + p2), (p0 + p1) + below))
        return sums

    def decoded(before, now):
        return [
            [silu(before[0][hp] + (now if tp else before)[1][hp] + now[2][hp] + bias) for hp in range(2)]
            for tp in range(2)
        ]

    first = LT // 2 * frame
    multiply(0, count * 2 // 3)
    sums = [over_rows(n * frame, upper_packed) for n in range(LT // 2)]
    wrapped = [
        [jnp.where(earlier, sums[0][kt][hp], turn(sums[-1][kt][hp], 6)) for hp in range(2)] for kt in range(2)
    ]
    others = [decoded(before, now) for before, now in zip([wrapped] + sums[:-1], sums)]
    before = None
    copies = []
    for t in range(LT):
        if first + t * frame == count * 2 // 3:
            multiply(count * 2 // 3, count - count * 2 // 3)
        now = over_rows(first + t * frame, upper_own)
        own = decoded(now if before is None else before, now)
        before = now
        for tp in range(2):
            blended = []
            for hp in range(2):
                other = others[t % (LT // 2)][tp][hp]
                if t >= LT // 2:
                    other = turn(other, 2)
                blended.append(own[tp][hp] * own_weight + other * other_weight)
            even, odd = blended
            at = (2 * t + tp) * 2 * frame
            out_ref[at:at + frame, :] = jnp.where(low, even, turn(odd, 4)).astype(jnp.bfloat16)
            out_ref[at + frame:at + 2 * frame, :] = jnp.where(low, turn(even, 4), odd).astype(jnp.bfloat16)
        both = pl.ds(t * 4 * frame, 4 * frame)
        copies.append(pltpu.make_async_copy(out_ref.at[both], out_hbm.at[both], sems.at[t]))
        copies[-1].start()
    for copy in copies:
        copy.wait()


def vmem():
    return pl.BlockSpec(memory_space=pltpu.VMEM)


def smem():
    return pl.BlockSpec(memory_space=pltpu.SMEM)


def hbm():
    return pl.BlockSpec(memory_space=pltpu.HBM)


def outside(value):
    return pltpu.with_memory_space_constraint(value, pltpu.HBM)


def held(value):
    return pltpu.with_memory_space_constraint(value, pltpu.VMEM)


def per_device(latent_rows, line_order, conv_weight, conv_bias, blend_table, blend_ids):
    tiles = lax.axis_size("tile")
    rows, depth = latent_rows.shape
    co = conv_weight.shape[-1]
    lines = line_order.shape[0]
    span = WD + 2
    weights = conv_weight.reshape(-1, co)
    frame = lines // LT * 4
    count = (LT + LT // 2) * frame
    order = [tile_of(place, tiles) for place in range(tiles)]
    position = lax.axis_index("tile").astype(jnp.int32).reshape(1)
    x, take, hot, mix, bias = pl.pallas_call(
        functools.partial(prepare_kernel, tiles),
        out_shape=(
            pltpu.VMEM((rows, depth), jnp.bfloat16),
            pltpu.VMEM((lines * span, rows), jnp.bfloat16),
            pltpu.VMEM((3, count, lines * span), jnp.bfloat16),
            pltpu.VMEM((2, 8, co), jnp.float32),
            pltpu.VMEM((1, co), jnp.float32),
        ),
        in_specs=[hbm()] * 5 + [smem()],
        out_specs=(vmem(),) * 5,
        scratch_shapes=[
            pltpu.VMEM((1, lines), jnp.int32),
            pltpu.SMEM(blend_ids.shape, jnp.int32),
            pltpu.SMEM(blend_table.shape, jnp.float32),
            pltpu.SemaphoreType.DMA((5,)),
        ],
    )(
        *map(outside, (latent_rows, line_order.reshape(1, -1), blend_ids, blend_table, conv_bias.reshape(1, co))),
        position,
    )
    send = pl.pallas_call(
        windows_kernel,
        out_shape=pltpu.VMEM((lines * span, depth), jnp.bfloat16),
        in_specs=[vmem(), vmem()],
        out_specs=vmem(),
        cost_estimate=pl.CostEstimate(flops=10**10, bytes_accessed=10**7, transcendentals=0),
    )(held(x), held(take))
    received = lax.all_to_all(send, "tile", 0, 0, axis_index_groups=[order], tiled=True)
    out = pl.pallas_call(
        decode_kernel,
        out_shape=jax.ShapeDtypeStruct((4 * LT * frame, co), jnp.bfloat16),
        in_specs=[vmem()] * 5,
        out_specs=hbm(),
        scratch_shapes=[
            pltpu.VMEM((9, count, co), jnp.float32),
            pltpu.VMEM((4 * LT * frame, co), jnp.bfloat16),
            pltpu.SemaphoreType.DMA((LT,)),
        ],
        compiler_params=pltpu.CompilerParams(vmem_limit_bytes=48 * 1024 * 1024),
    )(held(received), held(hot), weights, held(bias), held(mix))
    return out.reshape(2 * LT, lines // LT * 2, 2 * WD, co)


def solution(mesh):
    return jax.shard_map(
        per_device,
        mesh=mesh,
        in_specs=(P(("groups", "tile"), None), P("groups"), P(), P(), P(), P("groups")),
        out_specs=P("groups", None, "tile", None),
        check_vma=False,
    )
```

```python
import functools

import jax
import jax.numpy as jnp
from jax import lax
from jax.experimental import pallas as pl
from jax.experimental.pallas import tpu as pltpu
from jax.sharding import PartitionSpec as P

LT = 4
WD = 2
OWN = ((0, 1, 1, 2), (1, 1, 2, 2), (1, 2, 2, 3))
NEIGHBOUR = ((None, 1, None, None), (None, 1, 2, None), (None, None, 2, None))
NONE = 7
MEASURED = (11, 1, 15, 12, 6, 13, 10, 14, 4, 3, 8, 0, 5, 2, 7, 9)
PACKED = ((1, 0, 2), (0, 0, 1), (0, 0, 2), (1, 1, 1), (1, 1, 2), (0, 1, 1), (0, 1, 2), (1, 0, 1))


def pick(index, values):
    out = jnp.full(index.shape, NONE, jnp.int32)
    for at, value in enumerate(values):
        if value is not None:
            out = jnp.where(index == at, value, out)
    return out


def order_of(tiles):
    if tiles == len(MEASURED):
        return MEASURED
    return tuple((tiles + 3 * tiles // 4 - 1 - place) % tiles for place in range(tiles))


def dot(a, b):
    return jnp.dot(a, b, preferred_element_type=jnp.float32)


def windows_hot(tiles, rows_in, rows_out):
    width = tiles * WD
    span = WD + 2
    per_tile = rows_in // width * span
    row = lax.broadcasted_iota(jnp.int32, (rows_out, 1), 0)
    tile = pick(lax.div(row, per_tile), order_of(tiles))
    line = lax.div(lax.rem(row, per_tile), span)
    at = tile * WD - 1 + lax.rem(row, span)
    want = jnp.where((at >= 0) & (at < width), line * width + at, -1)
    col = lax.broadcasted_iota(jnp.int32, (rows_out, rows_in), 1)
    return (want == col).astype(jnp.bfloat16)


def line_key(tiles, order, cols):
    lines = order.shape[1]
    span = WD + 2
    per_tile = lines // tiles
    line_at = lax.div(lax.broadcasted_iota(jnp.int32, (1, cols), 1), span)
    line_at = pick(lax.div(line_at, per_tile), order_of(tiles)) * per_tile + lax.rem(line_at, per_tile)
    spread = lax.broadcasted_iota(jnp.int32, (lines, cols), 0) == line_at
    order = jnp.broadcast_to(order.astype(jnp.float32), (8, lines))
    order = jnp.dot(order, spread.astype(jnp.float32), precision=lax.Precision.HIGHEST)[:1]
    column = lax.rem(lax.broadcasted_iota(jnp.int32, (1, cols), 1), span)
    return order.astype(jnp.int32) * 8 + column


def blend_mix(tiles, at, ids_ref, table_ref, shape):
    own = ids_ref[at]
    lower = ids_ref[jnp.maximum(at - 1, 0)]
    upper = ids_ref[jnp.minimum(at + 1, tiles - 1)]
    has_lower = jnp.where(at > 0, 1.0, 0.0)
    has_upper = jnp.where(at < tiles - 1, 1.0, 0.0)
    wide = 2 * WD + 4
    neighbour = [has_lower * table_ref[lower, wide - 2], has_lower * table_ref[lower, wide - 1]]
    neighbour += [has_upper * table_ref[upper, 0], has_upper * table_ref[upper, 1]]
    mine = [table_ref[own, c] for c in range(2, wide - 2)]
    sub = lax.rem(lax.broadcasted_iota(jnp.int32, shape, 0), 4)
    other = jnp.zeros(shape, jnp.float32)
    same = jnp.zeros(shape, jnp.float32)
    for q in range(4):
        other = jnp.where(sub == q, neighbour[q], other)
        same = jnp.where(sub == q, mine[q], same)
    total = same + other
    differs = (sub == 1) | (sub == 2)
    return jnp.where(differs, same, total) / total, jnp.where(differs, other, 0.0) / total


def wanted_keys(rows, lines):
    height = lines // LT
    half = height // 2
    row = lax.broadcasted_iota(jnp.int32, (rows, 1), 0)
    sub = lax.rem(row, 8)
    group = lax.div(row, 8)
    packed = LT // 2 * half
    own = group >= packed
    group = jnp.where(own, group - packed, group)
    later, lower, column = (pick(sub, [entry[n] for entry in PACKED]) for n in range(3))
    frame = lax.div(group, half) + jnp.where(own, 0, later * (LT // 2))
    at = lax.rem(group, half) + half * jnp.where(own, lax.div(sub, 4), lower)
    column = jnp.where(own, lax.rem(sub, 4), column)
    line = (frame * height + at) * 8
    return [line + jnp.where(own, pick(column, OWN[kw]), pick(column, NEIGHBOUR[kw])) for kw in range(3)]


def prepare_kernel(
    tiles, x_hbm, order_hbm, ids_hbm, table_hbm, bias_hbm, at_ref,
    x_ref, take_ref, hot_ref, mix_ref, bias_ref, order_ref, ids_ref, table_ref, sems,
):
    moves = [
        (order_hbm, order_ref), (x_hbm, x_ref), (ids_hbm, ids_ref), (table_hbm, table_ref), (bias_hbm, bias_ref),
    ]
    copies = [pltpu.make_async_copy(a, b, sems.at[n]) for n, (a, b) in enumerate(moves)]
    for copy in copies:
        copy.start()
    take_ref[...] = windows_hot(tiles, *take_ref.shape[::-1])
    rows, cols = hot_ref.shape[1:]
    wants = wanted_keys(rows, order_ref.shape[1])
    copies[0].wait()
    key = jnp.broadcast_to(line_key(tiles, order_ref[...], cols), (rows, cols))
    for kw in range(3):
        hot_ref[kw] = (key == wants[kw]).astype(jnp.bfloat16)
    for copy in copies[2:]:
        copy.wait()
    mix_ref[0], mix_ref[1] = blend_mix(tiles, at_ref[0], ids_ref, table_ref, mix_ref.shape[1:])
    copies[1].wait()


def windows_kernel(x_ref, take_ref, send_ref):
    send_ref[...] = dot(take_ref[...], x_ref[...]).astype(jnp.bfloat16)


def turn(value, by):
    shape = value.shape
    return pltpu.roll(value.reshape(shape[0] // 8, 8, shape[1]), by, 1).reshape(shape)


def silu(value):
    return 0.5 * value * (1.0 + jnp.tanh(0.5 * value))


def decode_kernel(rows_ref, hot_ref, w_ref, bias_ref, mix_ref, out_hbm, part_ref, out_ref, sems):
    depth = rows_ref.shape[1]
    count = hot_ref.shape[1]
    co = w_ref.shape[1]
    tap = 3 * depth
    frame = count // (LT + LT // 2)
    groups = frame // 8
    rows = rows_ref[...]
    bias = bias_ref[...]
    sub = lax.rem(lax.broadcasted_iota(jnp.int32, (frame, co), 0), 8)
    low = sub < 4
    upper_own = low[:8]
    upper_packed = (sub[:8] < 3) | (sub[:8] == 7)
    earlier = lax.rem(sub, 4)
    earlier = (earlier == 1) | (earlier == 2)
    own_weight = jnp.concatenate([mix_ref[0]] * groups, axis=0)
    other_weight = jnp.concatenate([mix_ref[1]] * groups, axis=0)

    def multiply(at, size):
        here = slice(at, at + size)
        lhs = jnp.concatenate([dot(hot_ref[kw, here], rows).astype(jnp.bfloat16) for kw in range(3)], axis=1)
        for k in range(0, 9, 2):
            if k + 1 < 9:
                pair = [w_ref[n * tap:(n + 1) * tap, :] for n in (k, k + 1)]
                both = dot(lhs, jnp.concatenate(pair, axis=1))
                part_ref[k, here] = both[:, :co]
                part_ref[k + 1, here] = both[:, co:]
            else:
                part_ref[k, here] = dot(lhs, w_ref[k * tap:(k + 1) * tap, :])

    def over_rows(at, upper):
        sums = []
        for kt in range(3):
            p0, p1, p2 = (part_ref[kt * 3 + kh, at:at + frame, :] for kh in range(3))
            above = jnp.concatenate([jnp.where(upper, 0.0, turn(p0[-8:], 4)), p0[:-8]], axis=0)
            below = jnp.concatenate([p2[8:], jnp.where(upper, turn(p2[:8], 4), 0.0)], axis=0)
            sums.append((above + (p1 + p2), (p0 + p1) + below))
        return sums

    def decoded(before, now):
        return [
            [silu(before[0][hp] + (now if tp else before)[1][hp] + now[2][hp] + bias) for hp in range(2)]
            for tp in range(2)
        ]

    first = LT // 2 * frame
    multiply(0, count * 2 // 3)
    sums = [over_rows(n * frame, upper_packed) for n in range(LT // 2)]
    wrapped = [
        [jnp.where(earlier, sums[0][kt][hp], turn(sums[-1][kt][hp], 6)) for hp in range(2)] for kt in range(2)
    ]
    others = [decoded(before, now) for before, now in zip([wrapped] + sums[:-1], sums)]
    before = None
    copies = []
    for t in range(LT):
        if first + t * frame == count * 2 // 3:
            multiply(count * 2 // 3, count - count * 2 // 3)
        now = over_rows(first + t * frame, upper_own)
        own = decoded(now if before is None else before, now)
        before = now
        for tp in range(2):
            blended = []
            for hp in range(2):
                other = others[t % (LT // 2)][tp][hp]
                if t >= LT // 2:
                    other = turn(other, 2)
                blended.append(own[tp][hp] * own_weight + other * other_weight)
            even, odd = blended
            at = (2 * t + tp) * 2 * frame
            out_ref[at:at + frame, :] = jnp.where(low, even, turn(odd, 4)).astype(jnp.bfloat16)
            out_ref[at + frame:at + 2 * frame, :] = jnp.where(low, turn(even, 4), odd).astype(jnp.bfloat16)
        both = pl.ds(t * 4 * frame, 4 * frame)
        copies.append(pltpu.make_async_copy(out_ref.at[both], out_hbm.at[both], sems.at[t]))
        copies[-1].start()
    for copy in copies:
        copy.wait()


def vmem():
    return pl.BlockSpec(memory_space=pltpu.VMEM)


def smem():
    return pl.BlockSpec(memory_space=pltpu.SMEM)


def hbm():
    return pl.BlockSpec(memory_space=pltpu.HBM)


def outside(value):
    return pltpu.with_memory_space_constraint(value, pltpu.HBM)


def held(value):
    return pltpu.with_memory_space_constraint(value, pltpu.VMEM)


def per_device(latent_rows, line_order, conv_weight, conv_bias, blend_table, blend_ids):
    tiles = lax.axis_size("tile")
    rows, depth = latent_rows.shape
    co = conv_weight.shape[-1]
    lines = line_order.shape[0]
    span = WD + 2
    weights = conv_weight.reshape(-1, co)
    frame = lines // LT * 4
    count = (LT + LT // 2) * frame
    position = lax.axis_index("tile").astype(jnp.int32).reshape(1)
    x, take, hot, mix, bias = pl.pallas_call(
        functools.partial(prepare_kernel, tiles),
        out_shape=(
            pltpu.VMEM((rows, depth), jnp.bfloat16),
            pltpu.VMEM((lines * span, rows), jnp.bfloat16),
            pltpu.VMEM((3, count, lines * span), jnp.bfloat16),
            pltpu.VMEM((2, 8, co), jnp.float32),
            pltpu.VMEM((1, co), jnp.float32),
        ),
        in_specs=[hbm()] * 5 + [smem()],
        out_specs=(vmem(),) * 5,
        scratch_shapes=[
            pltpu.VMEM((1, lines), jnp.int32),
            pltpu.SMEM(blend_ids.shape, jnp.int32),
            pltpu.SMEM(blend_table.shape, jnp.float32),
            pltpu.SemaphoreType.DMA((5,)),
        ],
    )(
        *map(outside, (latent_rows, line_order.reshape(1, -1), blend_ids, blend_table, conv_bias.reshape(1, co))),
        position,
    )
    send = pl.pallas_call(
        windows_kernel,
        out_shape=pltpu.VMEM((lines * span, depth), jnp.bfloat16),
        in_specs=[vmem(), vmem()],
        out_specs=vmem(),
        cost_estimate=pl.CostEstimate(flops=10**10, bytes_accessed=10**7, transcendentals=0),
    )(held(x), held(take))
    received = lax.all_to_all(send, "tile", 0, 0, axis_index_groups=[list(order_of(tiles))], tiled=True)
    out = pl.pallas_call(
        decode_kernel,
        out_shape=jax.ShapeDtypeStruct((4 * LT * frame, co), jnp.bfloat16),
        in_specs=[vmem()] * 5,
        out_specs=hbm(),
        scratch_shapes=[
            pltpu.VMEM((9, count, co), jnp.float32),
            pltpu.VMEM((4 * LT * frame, co), jnp.bfloat16),
            pltpu.SemaphoreType.DMA((LT,)),
        ],
        compiler_params=pltpu.CompilerParams(vmem_limit_bytes=48 * 1024 * 1024),
    )(held(received), held(hot), weights, held(bias), held(mix))
    return out.reshape(2 * LT, lines // LT * 2, 2 * WD, co)


def solution(mesh):
    return jax.shard_map(
        per_device,
        mesh=mesh,
        in_specs=(P(("groups", "tile"), None), P("groups"), P(), P(), P(), P("groups")),
        out_specs=P("groups", None, "tile", None),
        check_vma=False,
    )
```

```python
import functools

import jax
import jax.numpy as jnp
from jax import lax
from jax.experimental import pallas as pl
from jax.experimental.pallas import tpu as pltpu
from jax.sharding import PartitionSpec as P

LT = 4
WD = 2
TAKES = ((0, 1, 1, 2), (1, 1, 2, 2), (1, 2, 2, 3))
MEASURED = (11, 1, 15, 12, 6, 13, 10, 14, 4, 3, 8, 0, 5, 2, 7, 9)
PACKED = ((1, 0, 2), (0, 0, 1), (0, 0, 2), (1, 1, 1), (1, 1, 2), (0, 1, 1), (0, 1, 2), (1, 0, 1))


def pick(index, values):
    out = jnp.full(index.shape, values[0], jnp.int32)
    for at, value in enumerate(values[1:], 1):
        out = jnp.where(index == at, value, out)
    return out


def order_of(tiles):
    if tiles == len(MEASURED):
        return MEASURED
    return tuple((tiles + 3 * tiles // 4 - 1 - place) % tiles for place in range(tiles))


def dot(a, b):
    return jnp.dot(a, b, preferred_element_type=jnp.float32)


def windows_hot(tiles, rows_in, rows_out):
    width = tiles * WD
    span = WD + 2
    per_tile = rows_in // width * span
    row = lax.broadcasted_iota(jnp.int32, (rows_out, 1), 0)
    tile = pick(lax.div(row, per_tile), order_of(tiles))
    line = lax.div(lax.rem(row, per_tile), span)
    at = tile * WD - 1 + lax.rem(row, span)
    want = jnp.where((at >= 0) & (at < width), line * width + at, -1)
    col = lax.broadcasted_iota(jnp.int32, (rows_out, rows_in), 1)
    return (want == col).astype(jnp.bfloat16)


def line_key(tiles, order, cols):
    lines = order.shape[1]
    span = WD + 2
    per_tile = lines // tiles
    line_at = lax.div(lax.broadcasted_iota(jnp.int32, (1, cols), 1), span)
    line_at = pick(lax.div(line_at, per_tile), order_of(tiles)) * per_tile + lax.rem(line_at, per_tile)
    spread = lax.broadcasted_iota(jnp.int32, (lines, cols), 0) == line_at
    digits = jnp.concatenate([lax.div(order, 128), lax.rem(order, 128)] * 4, axis=0)
    digits = dot(digits.astype(jnp.float32).astype(jnp.bfloat16), spread.astype(jnp.float32).astype(jnp.bfloat16))
    order = digits[:1] * 128.0 + digits[1:2]
    column = lax.rem(lax.broadcasted_iota(jnp.int32, (1, cols), 1), span)
    return order.astype(jnp.int32) * 8 + column


def blend_mix(tiles, at, ids_ref, table_ref, shape):
    own = ids_ref[at]
    lower = ids_ref[jnp.maximum(at - 1, 0)]
    upper = ids_ref[jnp.minimum(at + 1, tiles - 1)]
    has_lower = jnp.where(at > 0, 1.0, 0.0)
    has_upper = jnp.where(at < tiles - 1, 1.0, 0.0)
    wide = 2 * WD + 4
    neighbour = [has_lower * table_ref[lower, wide - 2], has_lower * table_ref[lower, wide - 1]]
    neighbour += [has_upper * table_ref[upper, 0], has_upper * table_ref[upper, 1]]
    mine = [table_ref[own, c] for c in range(2, wide - 2)]
    sub = lax.rem(lax.broadcasted_iota(jnp.int32, shape, 0), 4)
    other = jnp.zeros(shape, jnp.float32)
    same = jnp.zeros(shape, jnp.float32)
    for q in range(4):
        other = jnp.where(sub == q, neighbour[q], other)
        same = jnp.where(sub == q, mine[q], same)
    total = same + other
    differs = (sub == 1) | (sub == 2)
    return jnp.where(differs, same, total) / total, jnp.where(differs, other, 0.0) / total


def wanted_keys(rows, lines):
    height = lines // LT
    half = height // 2
    row = lax.broadcasted_iota(jnp.int32, (rows, 1), 0)
    sub = lax.rem(row, 8)
    group = lax.div(row, 8)
    at = lax.rem(group, half) + half * lax.div(sub, 4)
    line = (lax.div(group, half) * height + at) * 8
    return [line + pick(lax.rem(sub, 4), TAKES[kw]) for kw in range(3)]


def prepare_kernel(
    tiles, x_hbm, order_hbm, ids_hbm, table_hbm, bias_hbm, at_ref,
    x_ref, take_ref, hot_ref, mix_ref, bias_ref, order_ref, ids_ref, table_ref, sems,
):
    moves = [
        (order_hbm, order_ref), (x_hbm, x_ref), (ids_hbm, ids_ref), (table_hbm, table_ref), (bias_hbm, bias_ref),
    ]
    copies = [pltpu.make_async_copy(a, b, sems.at[n]) for n, (a, b) in enumerate(moves)]
    for copy in copies:
        copy.start()
    take_ref[...] = windows_hot(tiles, *take_ref.shape[::-1])
    rows, cols = hot_ref.shape[1:]
    wants = wanted_keys(rows, order_ref.shape[1])
    copies[0].wait()
    key = jnp.broadcast_to(line_key(tiles, order_ref[...], cols), (rows, cols))
    for kw in range(3):
        hot_ref[kw] = (key == wants[kw]).astype(jnp.bfloat16)
    for copy in copies[2:]:
        copy.wait()
    mix_ref[0], mix_ref[1] = blend_mix(tiles, at_ref[0], ids_ref, table_ref, mix_ref.shape[1:])
    copies[1].wait()


def windows_kernel(x_ref, take_ref, send_ref):
    send_ref[...] = dot(take_ref[...], x_ref[...]).astype(jnp.bfloat16)


def turn(value, by):
    shape = value.shape
    return pltpu.roll(value.reshape(shape[0] // 8, 8, shape[1]), by, 1).reshape(shape)


def silu(value):
    return 0.5 * value * (1.0 + jnp.tanh(0.5 * value))


def decode_kernel(rows_ref, hot_ref, w_ref, bias_ref, mix_ref, out_hbm, part_ref, out_ref, sems):
    depth = rows_ref.shape[1]
    count = hot_ref.shape[1]
    co = w_ref.shape[1]
    tap = 3 * depth
    frame = count // LT
    groups = frame // 8
    rows = rows_ref[...]
    bias = bias_ref[...]
    sub = lax.rem(lax.broadcasted_iota(jnp.int32, (frame, co), 0), 8)
    low = sub < 4
    own_weight = jnp.concatenate([mix_ref[0]] * groups, axis=0)
    other_weight = jnp.concatenate([mix_ref[1]] * groups, axis=0)

    def multiply(at, size):
        here = slice(at, at + size)
        left = [dot(hot_ref[kw, here], rows).astype(jnp.bfloat16) for kw in range(3)]
        for k in range(0, 9, 2):
            taps = range(k, min(k + 2, 9))
            r0, r1, r2 = (
                dot(left[kw], jnp.concatenate([w_ref[n * tap + kw * depth:n * tap + (kw + 1) * depth, :] for n in taps], axis=1))
                for kw in range(3)
            )
            first = lax.rem(lax.broadcasted_iota(jnp.int32, r0.shape, 0), 4) < 2
            own = r0 + r1 + r2
            other = r1 + jnp.where(first, r0, r2)
            for n in taps:
                lanes = slice((n - k) * co, (n - k + 1) * co)
                part_ref[0, n, here] = own[:, lanes]
                part_ref[1, n, here] = other[:, lanes]

    def over_rows(which, at):
        sums = []
        for kt in range(3):
            p0, p1, p2 = (part_ref[which, kt * 3 + kh, at:at + frame, :] for kh in range(3))
            above = jnp.concatenate([jnp.where(low[:8], 0.0, turn(p0[-8:], 4)), p0[:-8]], axis=0)
            below = jnp.concatenate([p2[8:], jnp.where(low[:8], turn(p2[:8], 4), 0.0)], axis=0)
            sums.append((above + (p1 + p2), (p0 + p1) + below))
        return sums

    def decoded(before, now):
        return [
            [silu(before[0][hp] + (now if tp else before)[1][hp] + now[2][hp] + bias) for hp in range(2)]
            for tp in range(2)
        ]

    before = None
    copies = []
    for t in range(LT):
        if t % 4 == 0:
            multiply(t * frame, 4 * frame)
        now = [over_rows(which, t * frame) for which in range(2)]
        own, other = (decoded(*pair) for pair in zip(now if before is None else before, now))
        before = now
        for tp in range(2):
            blended = [own[tp][hp] * own_weight + other[tp][hp] * other_weight for hp in range(2)]
            even, odd = blended
            at = (2 * t + tp) * 2 * frame
            out_ref[at:at + frame, :] = jnp.where(low, even, turn(odd, 4)).astype(jnp.bfloat16)
            out_ref[at + frame:at + 2 * frame, :] = jnp.where(low, turn(even, 4), odd).astype(jnp.bfloat16)
        both = pl.ds(t * 4 * frame, 4 * frame)
        copies.append(pltpu.make_async_copy(out_ref.at[both], out_hbm.at[both], sems.at[t]))
        copies[-1].start()
    for copy in copies:
        copy.wait()


def vmem():
    return pl.BlockSpec(memory_space=pltpu.VMEM)


def smem():
    return pl.BlockSpec(memory_space=pltpu.SMEM)


def hbm():
    return pl.BlockSpec(memory_space=pltpu.HBM)


def outside(value):
    return pltpu.with_memory_space_constraint(value, pltpu.HBM)


def held(value):
    return pltpu.with_memory_space_constraint(value, pltpu.VMEM)


def per_device(latent_rows, line_order, conv_weight, conv_bias, blend_table, blend_ids):
    tiles = lax.axis_size("tile")
    rows, depth = latent_rows.shape
    co = conv_weight.shape[-1]
    lines = line_order.shape[0]
    span = WD + 2
    weights = conv_weight.reshape(-1, co)
    frame = lines // LT * 4
    count = LT * frame
    position = lax.axis_index("tile").astype(jnp.int32).reshape(1)
    x, take, hot, mix, bias = pl.pallas_call(
        functools.partial(prepare_kernel, tiles),
        out_shape=(
            pltpu.VMEM((rows, depth), jnp.bfloat16),
            pltpu.VMEM((lines * span, rows), jnp.bfloat16),
            pltpu.VMEM((3, count, lines * span), jnp.bfloat16),
            pltpu.VMEM((2, 8, co), jnp.float32),
            pltpu.VMEM((1, co), jnp.float32),
        ),
        in_specs=[hbm()] * 5 + [smem()],
        out_specs=(vmem(),) * 5,
        scratch_shapes=[
            pltpu.VMEM((1, lines), jnp.int32),
            pltpu.SMEM(blend_ids.shape, jnp.int32),
            pltpu.SMEM(blend_table.shape, jnp.float32),
            pltpu.SemaphoreType.DMA((5,)),
        ],
    )(
        *map(outside, (latent_rows, line_order.reshape(1, -1), blend_ids, blend_table, conv_bias.reshape(1, co))),
        position,
    )
    send = pl.pallas_call(
        windows_kernel,
        out_shape=pltpu.VMEM((lines * span, depth), jnp.bfloat16),
        in_specs=[vmem(), vmem()],
        out_specs=vmem(),
        cost_estimate=pl.CostEstimate(flops=10**10, bytes_accessed=10**7, transcendentals=0),
    )(held(x), held(take))
    received = lax.all_to_all(send, "tile", 0, 0, axis_index_groups=[list(order_of(tiles))], tiled=True)
    out = pl.pallas_call(
        decode_kernel,
        out_shape=jax.ShapeDtypeStruct((4 * LT * frame, co), jnp.bfloat16),
        in_specs=[vmem()] * 5,
        out_specs=hbm(),
        scratch_shapes=[
            pltpu.VMEM((2, 9, count, co), jnp.float32),
            pltpu.VMEM((4 * LT * frame, co), jnp.bfloat16),
            pltpu.SemaphoreType.DMA((LT,)),
        ],
        compiler_params=pltpu.CompilerParams(vmem_limit_bytes=48 * 1024 * 1024),
    )(held(received), held(hot), weights, held(bias), held(mix))
    return out.reshape(2 * LT, lines // LT * 2, 2 * WD, co)


def solution(mesh):
    return jax.shard_map(
        per_device,
        mesh=mesh,
        in_specs=(P(("groups", "tile"), None), P("groups"), P(), P(), P(), P("groups")),
        out_specs=P("groups", None, "tile", None),
        check_vma=False,
    )
```

```python
import functools

import jax
import jax.numpy as jnp
from jax import lax
from jax.experimental import pallas as pl
from jax.experimental.pallas import tpu as pltpu
from jax.sharding import PartitionSpec as P

LT = 4
WD = 2
TAKES = ((0, 1, 1, 2), (1, 1, 2, 2), (1, 2, 2, 3))
MEASURED = (11, 1, 15, 12, 6, 13, 10, 14, 4, 3, 8, 0, 5, 2, 7, 9)
PACKED = ((1, 0, 2), (0, 0, 1), (0, 0, 2), (1, 1, 1), (1, 1, 2), (0, 1, 1), (0, 1, 2), (1, 0, 1))


def pick(index, values):
    out = jnp.full(index.shape, values[0], jnp.int32)
    for at, value in enumerate(values[1:], 1):
        out = jnp.where(index == at, value, out)
    return out


def order_of(tiles):
    if tiles == len(MEASURED):
        return MEASURED
    return tuple((tiles + 3 * tiles // 4 - 1 - place) % tiles for place in range(tiles))


def dot(a, b):
    return jnp.dot(a, b, preferred_element_type=jnp.float32)


def windows_hot(tiles, rows_in, rows_out):
    width = tiles * WD
    span = WD + 2
    per_tile = rows_in // width * span
    row = lax.broadcasted_iota(jnp.int32, (rows_out, 1), 0)
    tile = pick(lax.div(row, per_tile), order_of(tiles))
    line = lax.div(lax.rem(row, per_tile), span)
    at = tile * WD - 1 + lax.rem(row, span)
    want = jnp.where((at >= 0) & (at < width), line * width + at, -1)
    col = lax.broadcasted_iota(jnp.int32, (rows_out, rows_in), 1)
    return (want == col).astype(jnp.bfloat16)


def line_key(tiles, order, cols):
    lines = order.shape[1]
    span = WD + 2
    per_tile = lines // tiles
    line_at = lax.div(lax.broadcasted_iota(jnp.int32, (1, cols), 1), span)
    line_at = pick(lax.div(line_at, per_tile), order_of(tiles)) * per_tile + lax.rem(line_at, per_tile)
    spread = lax.broadcasted_iota(jnp.int32, (lines, cols), 0) == line_at
    digits = jnp.concatenate([lax.div(order, 128), lax.rem(order, 128)] * 4, axis=0)
    digits = dot(digits.astype(jnp.float32).astype(jnp.bfloat16), spread.astype(jnp.float32).astype(jnp.bfloat16))
    order = digits[:1] * 128.0 + digits[1:2]
    column = lax.rem(lax.broadcasted_iota(jnp.int32, (1, cols), 1), span)
    return order.astype(jnp.int32) * 8 + column


def blend_mix(tiles, at, ids_ref, table_ref, shape):
    own = ids_ref[at]
    lower = ids_ref[jnp.maximum(at - 1, 0)]
    upper = ids_ref[jnp.minimum(at + 1, tiles - 1)]
    has_lower = jnp.where(at > 0, 1.0, 0.0)
    has_upper = jnp.where(at < tiles - 1, 1.0, 0.0)
    wide = 2 * WD + 4
    neighbour = [has_lower * table_ref[lower, wide - 2], has_lower * table_ref[lower, wide - 1]]
    neighbour += [has_upper * table_ref[upper, 0], has_upper * table_ref[upper, 1]]
    mine = [table_ref[own, c] for c in range(2, wide - 2)]
    sub = lax.rem(lax.broadcasted_iota(jnp.int32, shape, 0), 4)
    other = jnp.zeros(shape, jnp.float32)
    same = jnp.zeros(shape, jnp.float32)
    for q in range(4):
        other = jnp.where(sub == q, neighbour[q], other)
        same = jnp.where(sub == q, mine[q], same)
    total = same + other
    differs = (sub == 1) | (sub == 2)
    return jnp.where(differs, same, total) / total, jnp.where(differs, other, 0.0) / total


def wanted_keys(rows, lines):
    height = lines // LT
    half = height // 2
    row = lax.broadcasted_iota(jnp.int32, (rows, 1), 0)
    sub = lax.rem(row, 8)
    group = lax.div(row, 8)
    at = lax.rem(group, half) + half * lax.div(sub, 4)
    line = (lax.div(group, half) * height + at) * 8
    return [line + pick(lax.rem(sub, 4), TAKES[kw]) for kw in range(3)]


def prepare_kernel(
    tiles, x_hbm, order_hbm, ids_hbm, table_hbm, bias_hbm, at_ref,
    x_ref, take_ref, hot_ref, mix_ref, bias_ref, order_ref, ids_ref, table_ref, sems,
):
    moves = [
        (ids_hbm, ids_ref), (table_hbm, table_ref), (order_hbm, order_ref), (x_hbm, x_ref), (bias_hbm, bias_ref),
    ]
    copies = [pltpu.make_async_copy(a, b, sems.at[n]) for n, (a, b) in enumerate(moves)]
    for copy in copies:
        copy.start()
    take_ref[...] = windows_hot(tiles, *take_ref.shape[::-1])
    rows, cols = hot_ref.shape[1:]
    wants = wanted_keys(rows, order_ref.shape[1])
    for copy in copies[:2]:
        copy.wait()
    mix_ref[0], mix_ref[1] = blend_mix(tiles, at_ref[0], ids_ref, table_ref, mix_ref.shape[1:])
    copies[2].wait()
    key = jnp.broadcast_to(line_key(tiles, order_ref[...], cols), (rows, cols))
    for kw in range(3):
        hot_ref[kw] = (key == wants[kw]).astype(jnp.bfloat16)
    copies[4].wait()
    copies[3].wait()


def windows_kernel(x_ref, take_ref, send_ref):
    send_ref[...] = dot(take_ref[...], x_ref[...]).astype(jnp.bfloat16)


def turn(value, by):
    shape = value.shape
    return pltpu.roll(value.reshape(shape[0] // 8, 8, shape[1]), by, 1).reshape(shape)


def silu(value):
    half = 0.5 * value
    return half + half * jnp.tanh(half)


def decode_kernel(rows_ref, hot_ref, w_ref, bias_ref, mix_ref, out_hbm, part_ref, out_ref, sems):
    depth = rows_ref.shape[1]
    count = hot_ref.shape[1]
    co = w_ref.shape[1]
    tap = 3 * depth
    frame = count // LT
    groups = frame // 8
    rows = rows_ref[...]
    bias = bias_ref[...]
    sub = lax.rem(lax.broadcasted_iota(jnp.int32, (frame, co), 0), 8)
    low = sub < 4
    own_weight = jnp.concatenate([mix_ref[0]] * groups, axis=0)
    other_weight = jnp.concatenate([mix_ref[1]] * groups, axis=0)

    def multiply(at, size):
        here = slice(at, at + size)
        left = [dot(hot_ref[kw, here], rows).astype(jnp.bfloat16) for kw in range(3)]
        for k in range(0, 9, 2):
            taps = range(k, min(k + 2, 9))
            r0, r1, r2 = (
                dot(left[kw], jnp.concatenate([w_ref[n * tap + kw * depth:n * tap + (kw + 1) * depth, :] for n in taps], axis=1))
                for kw in range(3)
            )
            first = lax.rem(lax.broadcasted_iota(jnp.int32, r0.shape, 0), 4) < 2
            own = r0 + r1 + r2
            other = r1 + jnp.where(first, r0, r2)
            for n in taps:
                lanes = slice((n - k) * co, (n - k + 1) * co)
                part_ref[0, n, here] = own[:, lanes]
                part_ref[1, n, here] = other[:, lanes]

    def over_rows(which, at):
        sums = []
        for kt in range(3):
            p0, p1, p2 = (part_ref[which, kt * 3 + kh, at:at + frame, :] for kh in range(3))
            above = jnp.concatenate([jnp.where(low[:8], 0.0, turn(p0[-8:], 4)), p0[:-8]], axis=0)
            below = jnp.concatenate([p2[8:], jnp.where(low[:8], turn(p2[:8], 4), 0.0)], axis=0)
            sums.append((above + (p1 + p2), (p0 + p1) + below))
        return sums

    def decoded(before, now):
        return [
            [silu(before[0][hp] + (now if tp else before)[1][hp] + now[2][hp] + bias) for hp in range(2)]
            for tp in range(2)
        ]

    before = None
    copies = []
    for t in range(LT):
        if t % 4 == 0:
            multiply(t * frame, 4 * frame)
        now = [over_rows(which, t * frame) for which in range(2)]
        own, other = (decoded(*pair) for pair in zip(now if before is None else before, now))
        before = now
        for tp in range(2):
            blended = [own[tp][hp] * own_weight + other[tp][hp] * other_weight for hp in range(2)]
            even, odd = blended
            at = (2 * t + tp) * 2 * frame
            out_ref[at:at + frame, :] = jnp.where(low, even, turn(odd, 4)).astype(jnp.bfloat16)
            out_ref[at + frame:at + 2 * frame, :] = jnp.where(low, turn(even, 4), odd).astype(jnp.bfloat16)
        both = pl.ds(t * 4 * frame, 4 * frame)
        copies.append(pltpu.make_async_copy(out_ref.at[both], out_hbm.at[both], sems.at[t]))
        copies[-1].start()
    for copy in copies:
        copy.wait()


def vmem():
    return pl.BlockSpec(memory_space=pltpu.VMEM)


def smem():
    return pl.BlockSpec(memory_space=pltpu.SMEM)


def hbm():
    return pl.BlockSpec(memory_space=pltpu.HBM)


def outside(value):
    return pltpu.with_memory_space_constraint(value, pltpu.HBM)


def held(value):
    return pltpu.with_memory_space_constraint(value, pltpu.VMEM)


def per_device(latent_rows, line_order, conv_weight, conv_bias, blend_table, blend_ids):
    tiles = lax.axis_size("tile")
    rows, depth = latent_rows.shape
    co = conv_weight.shape[-1]
    lines = line_order.shape[0]
    span = WD + 2
    weights = conv_weight.reshape(-1, co)
    frame = lines // LT * 4
    count = LT * frame
    position = lax.axis_index("tile").astype(jnp.int32).reshape(1)
    x, take, hot, mix, bias = pl.pallas_call(
        functools.partial(prepare_kernel, tiles),
        out_shape=(
            pltpu.VMEM((rows, depth), jnp.bfloat16),
            pltpu.VMEM((lines * span, rows), jnp.bfloat16),
            pltpu.VMEM((3, count, lines * span), jnp.bfloat16),
            pltpu.VMEM((2, 8, co), jnp.float32),
            pltpu.VMEM((1, co), jnp.float32),
        ),
        in_specs=[hbm()] * 5 + [smem()],
        out_specs=(vmem(),) * 5,
        scratch_shapes=[
            pltpu.VMEM((1, lines), jnp.int32),
            pltpu.SMEM(blend_ids.shape, jnp.int32),
            pltpu.SMEM(blend_table.shape, jnp.float32),
            pltpu.SemaphoreType.DMA((5,)),
        ],
    )(
        *map(outside, (latent_rows, line_order.reshape(1, -1), blend_ids, blend_table, conv_bias.reshape(1, co))),
        position,
    )
    send = pl.pallas_call(
        windows_kernel,
        out_shape=pltpu.VMEM((lines * span, depth), jnp.bfloat16),
        in_specs=[vmem(), vmem()],
        out_specs=vmem(),
        cost_estimate=pl.CostEstimate(flops=10**10, bytes_accessed=10**7, transcendentals=0),
    )(held(x), held(take))
    received = lax.all_to_all(send, "tile", 0, 0, axis_index_groups=[list(order_of(tiles))], tiled=True)
    out = pl.pallas_call(
        decode_kernel,
        out_shape=jax.ShapeDtypeStruct((4 * LT * frame, co), jnp.bfloat16),
        in_specs=[vmem()] * 5,
        out_specs=hbm(),
        scratch_shapes=[
            pltpu.VMEM((2, 9, count, co), jnp.float32),
            pltpu.VMEM((4 * LT * frame, co), jnp.bfloat16),
            pltpu.SemaphoreType.DMA((LT,)),
        ],
        compiler_params=pltpu.CompilerParams(vmem_limit_bytes=48 * 1024 * 1024),
    )(held(received), held(hot), weights, held(bias), held(mix))
    return out.reshape(2 * LT, lines // LT * 2, 2 * WD, co)


def solution(mesh):
    return jax.shard_map(
        per_device,
        mesh=mesh,
        in_specs=(P(("groups", "tile"), None), P("groups"), P(), P(), P(), P("groups")),
        out_specs=P("groups", None, "tile", None),
        check_vma=False,
    )
```

```python
import functools

import jax
import jax.numpy as jnp
from jax import lax
from jax.experimental import pallas as pl
from jax.experimental.pallas import tpu as pltpu
from jax.sharding import PartitionSpec as P

LT = 4
WD = 2
TAKES = ((0, 1, 1, 2), (1, 1, 2, 2), (1, 2, 2, 3))
MEASURED = (11, 1, 15, 12, 6, 13, 10, 14, 4, 3, 8, 0, 5, 2, 7, 9)
PACKED = ((1, 0, 2), (0, 0, 1), (0, 0, 2), (1, 1, 1), (1, 1, 2), (0, 1, 1), (0, 1, 2), (1, 0, 1))


def pick(index, values):
    out = jnp.full(index.shape, values[0], jnp.int32)
    for at, value in enumerate(values[1:], 1):
        out = jnp.where(index == at, value, out)
    return out


def order_of(tiles):
    if tiles == len(MEASURED):
        return MEASURED
    return tuple((tiles + 3 * tiles // 4 - 1 - place) % tiles for place in range(tiles))


def dot(a, b):
    return jnp.dot(a, b, preferred_element_type=jnp.float32)


def windows_hot(tiles, rows_in, rows_out):
    width = tiles * WD
    span = WD + 2
    per_tile = rows_in // width * span
    row = lax.broadcasted_iota(jnp.int32, (rows_out, 1), 0)
    tile = pick(lax.div(row, per_tile), order_of(tiles))
    line = lax.div(lax.rem(row, per_tile), span)
    at = tile * WD - 1 + lax.rem(row, span)
    want = jnp.where((at >= 0) & (at < width), line * width + at, -1)
    col = lax.broadcasted_iota(jnp.int32, (rows_out, rows_in), 1)
    return (want == col).astype(jnp.bfloat16)


def line_key(tiles, order, cols):
    lines = order.shape[1]
    span = WD + 2
    per_tile = lines // tiles
    line_at = lax.div(lax.broadcasted_iota(jnp.int32, (1, cols), 1), span)
    line_at = pick(lax.div(line_at, per_tile), order_of(tiles)) * per_tile + lax.rem(line_at, per_tile)
    spread = lax.broadcasted_iota(jnp.int32, (lines, cols), 0) == line_at
    digits = jnp.concatenate([lax.div(order, 128), lax.rem(order, 128)] * 4, axis=0)
    digits = dot(digits.astype(jnp.float32).astype(jnp.bfloat16), spread.astype(jnp.float32).astype(jnp.bfloat16))
    order = digits[:1] * 128.0 + digits[1:2]
    column = lax.rem(lax.broadcasted_iota(jnp.int32, (1, cols), 1), span)
    return order.astype(jnp.int32) * 8 + column


def blend_mix(tiles, at, ids_ref, table_ref, shape):
    own = ids_ref[at]
    lower = ids_ref[jnp.maximum(at - 1, 0)]
    upper = ids_ref[jnp.minimum(at + 1, tiles - 1)]
    has_lower = jnp.where(at > 0, 1.0, 0.0)
    has_upper = jnp.where(at < tiles - 1, 1.0, 0.0)
    wide = 2 * WD + 4
    neighbour = [has_lower * table_ref[lower, wide - 2], has_lower * table_ref[lower, wide - 1]]
    neighbour += [has_upper * table_ref[upper, 0], has_upper * table_ref[upper, 1]]
    mine = [table_ref[own, c] for c in range(2, wide - 2)]
    sub = lax.rem(lax.broadcasted_iota(jnp.int32, shape, 0), 4)
    other = jnp.zeros(shape, jnp.float32)
    same = jnp.zeros(shape, jnp.float32)
    for q in range(4):
        other = jnp.where(sub == q, neighbour[q], other)
        same = jnp.where(sub == q, mine[q], same)
    total = same + other
    differs = (sub == 1) | (sub == 2)
    return jnp.where(differs, same, total) / total, jnp.where(differs, other, 0.0) / total


def wanted_keys(rows, lines):
    height = lines // LT
    half = height // 2
    row = lax.broadcasted_iota(jnp.int32, (rows, 1), 0)
    sub = lax.rem(row, 8)
    group = lax.div(row, 8)
    at = lax.rem(group, half) + half * lax.div(sub, 4)
    line = (lax.div(group, half) * height + at) * 8
    return [line + pick(lax.rem(sub, 4), TAKES[kw]) for kw in range(3)]


def prepare_kernel(
    tiles, x_hbm, order_hbm, ids_hbm, table_hbm, at_ref,
    x_ref, take_ref, hot_ref, mix_ref, order_ref, ids_ref, table_ref, sems,
):
    moves = [
        (ids_hbm, ids_ref), (table_hbm, table_ref), (order_hbm, order_ref), (x_hbm, x_ref),
    ]
    copies = [pltpu.make_async_copy(a, b, sems.at[n]) for n, (a, b) in enumerate(moves)]
    for copy in copies:
        copy.start()
    take_ref[...] = windows_hot(tiles, *take_ref.shape[::-1])
    rows, cols = hot_ref.shape[1:]
    wants = wanted_keys(rows, order_ref.shape[1])
    for copy in copies[:2]:
        copy.wait()
    mix_ref[0], mix_ref[1] = blend_mix(tiles, at_ref[0], ids_ref, table_ref, mix_ref.shape[1:])
    copies[2].wait()
    key = jnp.broadcast_to(line_key(tiles, order_ref[...], cols), (rows, cols))
    for kw in range(3):
        hot_ref[kw] = (key == wants[kw]).astype(jnp.bfloat16)
    copies[3].wait()


def windows_kernel(x_ref, take_ref, send_ref):
    send_ref[...] = dot(take_ref[...], x_ref[...]).astype(jnp.bfloat16)


def turn(value, by):
    shape = value.shape
    return pltpu.roll(value.reshape(shape[0] // 8, 8, shape[1]), by, 1).reshape(shape)


def silu(value):
    half = 0.5 * value
    return half + half * jnp.tanh(half)


def decode_kernel(rows_ref, hot_ref, w_ref, bias_ref, mix_ref, out_hbm, part_ref, out_ref, sems):
    depth = rows_ref.shape[1]
    count = hot_ref.shape[1]
    co = w_ref.shape[1]
    tap = 3 * depth
    frame = count // LT
    groups = frame // 8
    rows = rows_ref[...]
    bias = bias_ref[...]
    sub = lax.rem(lax.broadcasted_iota(jnp.int32, (frame, co), 0), 8)
    low = sub < 4
    own_weight = jnp.concatenate([mix_ref[0]] * groups, axis=0)
    other_weight = jnp.concatenate([mix_ref[1]] * groups, axis=0)

    def multiply(at, size):
        here = slice(at, at + size)
        left = [dot(hot_ref[kw, here], rows).astype(jnp.bfloat16) for kw in range(3)]
        for k in range(0, 9, 2):
            taps = range(k, min(k + 2, 9))
            r0, r1, r2 = (
                dot(left[kw], jnp.concatenate([w_ref[n * tap + kw * depth:n * tap + (kw + 1) * depth, :] for n in taps], axis=1))
                for kw in range(3)
            )
            first = lax.rem(lax.broadcasted_iota(jnp.int32, r0.shape, 0), 4) < 2
            own = r0 + r1 + r2
            other = r1 + jnp.where(first, r0, r2)
            for n in taps:
                lanes = slice((n - k) * co, (n - k + 1) * co)
                part_ref[0, n, here] = own[:, lanes]
                part_ref[1, n, here] = other[:, lanes]

    def over_rows(which, at):
        sums = []
        for kt in range(3):
            p0, p1, p2 = (part_ref[which, kt * 3 + kh, at:at + frame, :] for kh in range(3))
            above = jnp.concatenate([jnp.where(low[:8], 0.0, turn(p0[-8:], 4)), p0[:-8]], axis=0)
            below = jnp.concatenate([p2[8:], jnp.where(low[:8], turn(p2[:8], 4), 0.0)], axis=0)
            sums.append((above + (p1 + p2), (p0 + p1) + below))
        return sums

    def decoded(before, now):
        return [
            [silu(before[0][hp] + (now if tp else before)[1][hp] + now[2][hp] + bias) for hp in range(2)]
            for tp in range(2)
        ]

    before = None
    copies = []
    for t in range(LT):
        if t % 4 == 0:
            multiply(t * frame, 4 * frame)
        now = [over_rows(which, t * frame) for which in range(2)]
        own, other = (decoded(*pair) for pair in zip(now if before is None else before, now))
        before = now
        for tp in range(2):
            blended = [own[tp][hp] * own_weight + other[tp][hp] * other_weight for hp in range(2)]
            even, odd = blended
            at = (2 * t + tp) * 2 * frame
            out_ref[at:at + frame, :] = jnp.where(low, even, turn(odd, 4)).astype(jnp.bfloat16)
            out_ref[at + frame:at + 2 * frame, :] = jnp.where(low, turn(even, 4), odd).astype(jnp.bfloat16)
        both = pl.ds(t * 4 * frame, 4 * frame)
        copies.append(pltpu.make_async_copy(out_ref.at[both], out_hbm.at[both], sems.at[t]))
        copies[-1].start()
    for copy in copies:
        copy.wait()


def vmem():
    return pl.BlockSpec(memory_space=pltpu.VMEM)


def smem():
    return pl.BlockSpec(memory_space=pltpu.SMEM)


def hbm():
    return pl.BlockSpec(memory_space=pltpu.HBM)


def outside(value):
    return pltpu.with_memory_space_constraint(value, pltpu.HBM)


def held(value):
    return pltpu.with_memory_space_constraint(value, pltpu.VMEM)


def per_device(latent_rows, line_order, conv_weight, conv_bias, blend_table, blend_ids):
    tiles = lax.axis_size("tile")
    rows, depth = latent_rows.shape
    co = conv_weight.shape[-1]
    lines = line_order.shape[0]
    span = WD + 2
    weights = conv_weight.reshape(-1, co)
    frame = lines // LT * 4
    count = LT * frame
    position = lax.axis_index("tile").astype(jnp.int32).reshape(1)
    x, take, hot, mix = pl.pallas_call(
        functools.partial(prepare_kernel, tiles),
        out_shape=(
            pltpu.VMEM((rows, depth), jnp.bfloat16),
            pltpu.VMEM((lines * span, rows), jnp.bfloat16),
            pltpu.VMEM((3, count, lines * span), jnp.bfloat16),
            pltpu.VMEM((2, 8, co), jnp.float32),
        ),
        in_specs=[hbm()] * 4 + [smem()],
        out_specs=(vmem(),) * 4,
        scratch_shapes=[
            pltpu.VMEM((1, lines), jnp.int32),
            pltpu.SMEM(blend_ids.shape, jnp.int32),
            pltpu.SMEM(blend_table.shape, jnp.float32),
            pltpu.SemaphoreType.DMA((4,)),
        ],
    )(
        *map(outside, (latent_rows, line_order.reshape(1, -1), blend_ids, blend_table)),
        position,
    )
    send = pl.pallas_call(
        windows_kernel,
        out_shape=pltpu.VMEM((lines * span, depth), jnp.bfloat16),
        in_specs=[vmem(), vmem()],
        out_specs=vmem(),
        cost_estimate=pl.CostEstimate(flops=10**10, bytes_accessed=10**7, transcendentals=0),
    )(held(x), held(take))
    received = lax.all_to_all(send, "tile", 0, 0, axis_index_groups=[list(order_of(tiles))], tiled=True)
    out = pl.pallas_call(
        decode_kernel,
        out_shape=jax.ShapeDtypeStruct((4 * LT * frame, co), jnp.bfloat16),
        in_specs=[vmem()] * 5,
        out_specs=hbm(),
        scratch_shapes=[
            pltpu.VMEM((2, 9, count, co), jnp.float32),
            pltpu.VMEM((4 * LT * frame, co), jnp.bfloat16),
            pltpu.SemaphoreType.DMA((LT,)),
        ],
        compiler_params=pltpu.CompilerParams(vmem_limit_bytes=48 * 1024 * 1024),
    )(held(received), held(hot), weights, conv_bias.reshape(1, co), held(mix))
    return out.reshape(2 * LT, lines // LT * 2, 2 * WD, co)


def solution(mesh):
    return jax.shard_map(
        per_device,
        mesh=mesh,
        in_specs=(P(("groups", "tile"), None), P("groups"), P(), P(), P(), P("groups")),
        out_specs=P("groups", None, "tile", None),
        check_vma=False,
    )
```

```python
import functools

import jax
import jax.numpy as jnp
from jax import lax
from jax.experimental import pallas as pl
from jax.experimental.pallas import tpu as pltpu
from jax.sharding import PartitionSpec as P

LT = 4
WD = 2
TAKES = ((0, 1, 1, 2), (1, 1, 2, 2), (1, 2, 2, 3))
MEASURED = (11, 1, 15, 12, 2, 13, 4, 14, 10, 3, 8, 0, 5, 6, 7, 9)
PACKED = ((1, 0, 2), (0, 0, 1), (0, 0, 2), (1, 1, 1), (1, 1, 2), (0, 1, 1), (0, 1, 2), (1, 0, 1))


def pick(index, values):
    out = jnp.full(index.shape, values[0], jnp.int32)
    for at, value in enumerate(values[1:], 1):
        out = jnp.where(index == at, value, out)
    return out


def order_of(tiles):
    if tiles == len(MEASURED):
        return MEASURED
    return tuple((tiles + 3 * tiles // 4 - 1 - place) % tiles for place in range(tiles))


def dot(a, b):
    return jnp.dot(a, b, preferred_element_type=jnp.float32)


def windows_hot(tiles, rows_in, rows_out):
    width = tiles * WD
    span = WD + 2
    per_tile = rows_in // width * span
    row = lax.broadcasted_iota(jnp.int32, (rows_out, 1), 0)
    tile = pick(lax.div(row, per_tile), order_of(tiles))
    line = lax.div(lax.rem(row, per_tile), span)
    at = tile * WD - 1 + lax.rem(row, span)
    want = jnp.where((at >= 0) & (at < width), line * width + at, -1)
    col = lax.broadcasted_iota(jnp.int32, (rows_out, rows_in), 1)
    return (want == col).astype(jnp.bfloat16)


def line_key(tiles, order, cols):
    lines = order.shape[1]
    span = WD + 2
    per_tile = lines // tiles
    line_at = lax.div(lax.broadcasted_iota(jnp.int32, (1, cols), 1), span)
    line_at = pick(lax.div(line_at, per_tile), order_of(tiles)) * per_tile + lax.rem(line_at, per_tile)
    spread = lax.broadcasted_iota(jnp.int32, (lines, cols), 0) == line_at
    digits = jnp.concatenate([lax.div(order, 128), lax.rem(order, 128)] * 4, axis=0)
    digits = dot(digits.astype(jnp.float32).astype(jnp.bfloat16), spread.astype(jnp.float32).astype(jnp.bfloat16))
    order = digits[:1] * 128.0 + digits[1:2]
    column = lax.rem(lax.broadcasted_iota(jnp.int32, (1, cols), 1), span)
    return order.astype(jnp.int32) * 8 + column


def blend_mix(tiles, at, ids_ref, table_ref, shape):
    own = ids_ref[at]
    lower = ids_ref[jnp.maximum(at - 1, 0)]
    upper = ids_ref[jnp.minimum(at + 1, tiles - 1)]
    has_lower = jnp.where(at > 0, 1.0, 0.0)
    has_upper = jnp.where(at < tiles - 1, 1.0, 0.0)
    wide = 2 * WD + 4
    neighbour = [has_lower * table_ref[lower, wide - 2], has_lower * table_ref[lower, wide - 1]]
    neighbour += [has_upper * table_ref[upper, 0], has_upper * table_ref[upper, 1]]
    mine = [table_ref[own, c] for c in range(2, wide - 2)]
    sub = lax.rem(lax.broadcasted_iota(jnp.int32, shape, 0), 4)
    other = jnp.zeros(shape, jnp.float32)
    same = jnp.zeros(shape, jnp.float32)
    for q in range(4):
        other = jnp.where(sub == q, neighbour[q], other)
        same = jnp.where(sub == q, mine[q], same)
    total = same + other
    differs = (sub == 1) | (sub == 2)
    return jnp.where(differs, same, total) / total, jnp.where(differs, other, 0.0) / total


def wanted_keys(rows, lines):
    height = lines // LT
    half = height // 2
    row = lax.broadcasted_iota(jnp.int32, (rows, 1), 0)
    sub = lax.rem(row, 8)
    group = lax.div(row, 8)
    at = lax.rem(group, half) + half * lax.div(sub, 4)
    line = (lax.div(group, half) * height + at) * 8
    return [line + pick(lax.rem(sub, 4), TAKES[kw]) for kw in range(3)]


def prepare_kernel(
    tiles, x_hbm, order_hbm, ids_hbm, table_hbm, at_ref,
    x_ref, take_ref, hot_ref, mix_ref, order_ref, ids_ref, table_ref, sems,
):
    moves = [
        (ids_hbm, ids_ref), (table_hbm, table_ref), (order_hbm, order_ref), (x_hbm, x_ref),
    ]
    copies = [pltpu.make_async_copy(a, b, sems.at[n]) for n, (a, b) in enumerate(moves)]
    for copy in copies:
        copy.start()
    take_ref[...] = windows_hot(tiles, *take_ref.shape[::-1])
    rows, cols = hot_ref.shape[1:]
    wants = wanted_keys(rows, order_ref.shape[1])
    for copy in copies[:2]:
        copy.wait()
    mix_ref[0], mix_ref[1] = blend_mix(tiles, at_ref[0], ids_ref, table_ref, mix_ref.shape[1:])
    copies[2].wait()
    key = jnp.broadcast_to(line_key(tiles, order_ref[...], cols), (rows, cols))
    for kw in range(3):
        hot_ref[kw] = (key == wants[kw]).astype(jnp.bfloat16)
    copies[3].wait()


def windows_kernel(x_ref, take_ref, send_ref):
    send_ref[...] = dot(take_ref[...], x_ref[...]).astype(jnp.bfloat16)


def turn(value, by):
    shape = value.shape
    return pltpu.roll(value.reshape(shape[0] // 8, 8, shape[1]), by, 1).reshape(shape)


def silu(value):
    half = 0.5 * value
    return half + half * jnp.tanh(half)


def decode_kernel(rows_ref, hot_ref, w_ref, bias_ref, mix_ref, out_hbm, part_ref, out_ref, sems):
    depth = rows_ref.shape[1]
    count = hot_ref.shape[1]
    co = w_ref.shape[1]
    tap = 3 * depth
    frame = count // LT
    groups = frame // 8
    rows = rows_ref[...]
    bias = bias_ref[...]
    sub = lax.rem(lax.broadcasted_iota(jnp.int32, (frame, co), 0), 8)
    low = sub < 4
    own_weight = jnp.concatenate([mix_ref[0]] * groups, axis=0)
    other_weight = jnp.concatenate([mix_ref[1]] * groups, axis=0)

    def multiply(at, size):
        here = slice(at, at + size)
        left = [dot(hot_ref[kw, here], rows).astype(jnp.bfloat16) for kw in range(3)]
        for k in range(0, 9, 2):
            taps = range(k, min(k + 2, 9))
            r0, r1, r2 = (
                dot(left[kw], jnp.concatenate([w_ref[n * tap + kw * depth:n * tap + (kw + 1) * depth, :] for n in taps], axis=1))
                for kw in range(3)
            )
            first = lax.rem(lax.broadcasted_iota(jnp.int32, r0.shape, 0), 4) < 2
            own = r0 + r1 + r2
            other = r1 + jnp.where(first, r0, r2)
            for n in taps:
                lanes = slice((n - k) * co, (n - k + 1) * co)
                part_ref[0, n, here] = own[:, lanes]
                part_ref[1, n, here] = other[:, lanes]

    def over_rows(which, at):
        sums = []
        for kt in range(3):
            p0, p1, p2 = (part_ref[which, kt * 3 + kh, at:at + frame, :] for kh in range(3))
            above = jnp.concatenate([jnp.where(low[:8], 0.0, turn(p0[-8:], 4)), p0[:-8]], axis=0)
            below = jnp.concatenate([p2[8:], jnp.where(low[:8], turn(p2[:8], 4), 0.0)], axis=0)
            sums.append((above + (p1 + p2), (p0 + p1) + below))
        return sums

    def decoded(before, now):
        return [
            [silu(before[0][hp] + (now if tp else before)[1][hp] + now[2][hp] + bias) for hp in range(2)]
            for tp in range(2)
        ]

    before = None
    copies = []
    for t in range(LT):
        if t % 4 == 0:
            multiply(t * frame, 4 * frame)
        now = [over_rows(which, t * frame) for which in range(2)]
        own, other = (decoded(*pair) for pair in zip(now if before is None else before, now))
        before = now
        for tp in range(2):
            blended = [own[tp][hp] * own_weight + other[tp][hp] * other_weight for hp in range(2)]
            even, odd = blended
            at = (2 * t + tp) * 2 * frame
            out_ref[at:at + frame, :] = jnp.where(low, even, turn(odd, 4)).astype(jnp.bfloat16)
            out_ref[at + frame:at + 2 * frame, :] = jnp.where(low, turn(even, 4), odd).astype(jnp.bfloat16)
        both = pl.ds(t * 4 * frame, 4 * frame)
        copies.append(pltpu.make_async_copy(out_ref.at[both], out_hbm.at[both], sems.at[t]))
        copies[-1].start()
    for copy in copies:
        copy.wait()


def vmem():
    return pl.BlockSpec(memory_space=pltpu.VMEM)


def smem():
    return pl.BlockSpec(memory_space=pltpu.SMEM)


def hbm():
    return pl.BlockSpec(memory_space=pltpu.HBM)


def outside(value):
    return pltpu.with_memory_space_constraint(value, pltpu.HBM)


def held(value):
    return pltpu.with_memory_space_constraint(value, pltpu.VMEM)


def per_device(latent_rows, line_order, conv_weight, conv_bias, blend_table, blend_ids):
    tiles = lax.axis_size("tile")
    rows, depth = latent_rows.shape
    co = conv_weight.shape[-1]
    lines = line_order.shape[0]
    span = WD + 2
    weights = conv_weight.reshape(-1, co)
    frame = lines // LT * 4
    count = LT * frame
    position = lax.axis_index("tile").astype(jnp.int32).reshape(1)
    x, take, hot, mix = pl.pallas_call(
        functools.partial(prepare_kernel, tiles),
        out_shape=(
            pltpu.VMEM((rows, depth), jnp.bfloat16),
            pltpu.VMEM((lines * span, rows), jnp.bfloat16),
            pltpu.VMEM((3, count, lines * span), jnp.bfloat16),
            pltpu.VMEM((2, 8, co), jnp.float32),
        ),
        in_specs=[hbm()] * 4 + [smem()],
        out_specs=(vmem(),) * 4,
        scratch_shapes=[
            pltpu.VMEM((1, lines), jnp.int32),
            pltpu.SMEM(blend_ids.shape, jnp.int32),
            pltpu.SMEM(blend_table.shape, jnp.float32),
            pltpu.SemaphoreType.DMA((4,)),
        ],
    )(
        *map(outside, (latent_rows, line_order.reshape(1, -1), blend_ids, blend_table)),
        position,
    )
    send = pl.pallas_call(
        windows_kernel,
        out_shape=pltpu.VMEM((lines * span, depth), jnp.bfloat16),
        in_specs=[vmem(), vmem()],
        out_specs=vmem(),
        cost_estimate=pl.CostEstimate(flops=10**10, bytes_accessed=10**7, transcendentals=0),
    )(held(x), held(take))
    received = lax.all_to_all(send, "tile", 0, 0, axis_index_groups=[list(order_of(tiles))], tiled=True)
    out = pl.pallas_call(
        decode_kernel,
        out_shape=jax.ShapeDtypeStruct((4 * LT * frame, co), jnp.bfloat16),
        in_specs=[vmem()] * 5,
        out_specs=hbm(),
        scratch_shapes=[
            pltpu.VMEM((2, 9, count, co), jnp.float32),
            pltpu.VMEM((4 * LT * frame, co), jnp.bfloat16),
            pltpu.SemaphoreType.DMA((LT,)),
        ],
        compiler_params=pltpu.CompilerParams(vmem_limit_bytes=48 * 1024 * 1024),
    )(held(received), held(hot), weights, conv_bias.reshape(1, co), held(mix))
    return out.reshape(2 * LT, lines // LT * 2, 2 * WD, co)


def solution(mesh):
    return jax.shard_map(
        per_device,
        mesh=mesh,
        in_specs=(P(("groups", "tile"), None), P("groups"), P(), P(), P(), P("groups")),
        out_specs=P("groups", None, "tile", None),
        check_vma=False,
    )
```
